256 devices in a mesh: conf: 64 (over z, x, core), state: 4 (over y).
Axes of the slice: x: 4, y: 4, z: 8, core: 2. Of those that a mesh axis runs over, the one named last changes fastest.
Arguments:
- energies: float32 [4096, 131072], P('state', 'conf'), may hold values from -160 to 160
- samples: int32 [4096], P('state'), may hold values from 1 to 63
- counts: int32 [32, 131072], P(None, 'conf'), may hold values from 0 to 2
- initial: float32 [32, 4096], P(None, 'state'), may hold values from -160 to 160
Outputs:
- free_energy: float32 [32, 4096], P(None, 'state')
- log_weight: float32 [32, 131072], P(None, 'conf')
The draws below stay inside these ranges and needn't reach their ends.
All inputs are finite; a program needn't handle non-finite values.
Results may differ from the reference program's by a relative error of at most 0.0003.
Values sent between devices are 32-bit elements; how exact they have to be, the bound alone decides.
A program may use at most 64 MiB of HBM per device.

```python
import math
import jax
import jax.numpy as jnp
from jax import lax

K = 4096
B = 32
ITERS = 2
CONFS = 131072


def draw_energies(key, part):
    key = jax.random.fold_in(key, 11)
    first, second = jax.random.split(key)
    base = jax.random.uniform(first, (1, CONFS), jnp.float32, -5.0, 5.0)
    rough = jnp.clip(2.0 * jax.random.normal(second, (K, CONFS), jnp.float32), -10.0, 10.0)
    return base + rough


def draw_initial(key, part):
    key = jax.random.fold_in(key, 23)
    second = jax.random.fold_in(key, 1)
    return jnp.clip(jax.random.normal(second, (B, K), jnp.float32), -4.0, 4.0)


def touch_ends(result, key, low, high):
    longest = result.shape.index(max(result.shape))
    spots = []
    for shift in (0, 1):
        where = [jax.random.randint(jax.random.fold_in(key, axis), (), 0, length) for axis, length in enumerate(result.shape)]
        where[longest] = (where[longest] + shift) % result.shape[longest]
        spots.append(tuple(where))
    return result.at[spots[0]].set(low).at[spots[1]].set(high)


def setup_inputs(seed: int = 0) -> dict:
    splits = jax.random.split(jax.random.key(seed), 5)
    return {
        "energies": draw_energies(jax.random.fold_in(splits[4], 71), 0),
        "samples": touch_ends(jax.random.randint(splits[1], (K,), 1, 64), jax.random.fold_in(splits[1], 1), 1, 63).astype(jnp.int32),
        "counts": touch_ends(jax.random.randint(splits[2], (B, CONFS), 0, 3), jax.random.fold_in(splits[2], 1), 0, 2).astype(jnp.int32),
        "initial": draw_initial(jax.random.fold_in(splits[4], 71), 0),
    }


def reference(energies, samples, counts, initial):
    width = math.gcd(CONFS, 4096)
    blocks = CONFS // width
    log_samples = jnp.log(samples.astype(jnp.float32))
    weight = counts.astype(jnp.float32)
    starts = jnp.arange(blocks, dtype=jnp.int32) * width

    def boltz_block(start):
        block = lax.dynamic_slice_in_dim(energies, start, width, 1)
        shift = jnp.max(-block, axis=0)
        return jnp.exp(-block - shift[None, :])

    free = initial
    denoms = None
    top = None
    for step in range(ITERS):
        lifted = log_samples[None, :] + free
        top = jnp.max(lifted, axis=1)
        scaled = jnp.exp(lifted - top[:, None])

        def visit(total, start):
            boltz = boltz_block(start)
            denom = jnp.dot(scaled, boltz, precision=lax.Precision.HIGHEST)
            ratio = lax.dynamic_slice_in_dim(weight, start, width, 1) / denom
            total = total + lax.dot_general(ratio, boltz, (((1,), (1,)), ((), ())), precision=lax.Precision.HIGHEST)
            return total, denom

        total, denoms = lax.scan(visit, jnp.zeros((B, K), jnp.float32), starts)
        value = top[:, None] - jnp.log(total)
        free = value - value[:, 0:1]
    denom_all = jnp.moveaxis(denoms, 0, 1).reshape(B, CONFS)
    log_weight = jnp.log(denom_all) + top[:, None]
    return free, log_weight
```

```python
import functools

import jax
import jax.numpy as jnp
from jax import lax
from jax.experimental import pallas as pl
from jax.experimental.pallas import tpu as pltpu
from jax.sharding import PartitionSpec as P

MESH = pl.DeviceIdType.MESH
ITERS = 2
B = 32
KS = 1024
NS = 2048
PIECES = 4
W = NS // PIECES
LOADS = 8
LW = NS // LOADS
GROUP = 8
RING = 8
F32 = jnp.float32
BF16 = jnp.bfloat16


def pack(column):
    lane = lax.broadcasted_iota(jnp.int32, (8, 128), 1) // 32
    out = jnp.broadcast_to(column[24:32], (8, 128))
    for j in (2, 1, 0):
        out = jnp.where(lane == j, jnp.broadcast_to(column[8 * j : 8 * j + 8], (8, 128)), out)
    return out


def unpack(tile):
    return jnp.concatenate([tile[:, 32 * j : 32 * j + 1] for j in range(4)], axis=0)


def split(x):
    high = x.astype(BF16)
    low = (x - high.astype(F32)).astype(BF16)
    return high, low


def kernel(
    e_hbm, samples_hbm, counts_hbm, initial_hbm, free_ref, lw_ref,
    e_buf, bh, bl, samples, counts, lifted, lhs, rhs, total, mine, log_samples,
    part1, part2, got1, got2, ext, ext_got, rows, rows_got, tot, tot_got, ring, ring_got, val, val_got,
    load_sem, small_sem, send_sem, recv_sem,
):
    c = lax.axis_index("conf")
    y = lax.axis_index("state")
    z, g = c // GROUP, c % GROUP
    peers = (y + 1 - 2 * (y % 2), 3 - y, (y + 2) % 4)

    loads = []
    small = [
        pltpu.make_async_copy(samples_hbm, samples, small_sem.at[0]),
        pltpu.make_async_copy(initial_hbm, lifted, small_sem.at[1]),
        pltpu.make_async_copy(counts_hbm, counts, small_sem.at[2]),
    ]
    small[0].start()
    small[1].start()
    for i in range(LOADS):
        copy = pltpu.make_async_copy(e_hbm.at[:, pl.ds(i * LW, LW)], e_buf.at[i], load_sem.at[i])
        copy.start()
        loads.append(copy)
    small[2].start()

    barrier = pltpu.get_barrier_semaphore()
    for peer in peers:
        pl.semaphore_signal(barrier, inc=1, device_id={"conf": c, "state": peer}, device_id_type=MESH)
    for o in range(1, GROUP):
        peer = z * GROUP + (g + o) % GROUP
        pl.semaphore_signal(barrier, inc=1, device_id={"conf": peer, "state": y}, device_id_type=MESH)
    for o in range(1, RING):
        peer = ((z + o) % RING) * GROUP + g
        pl.semaphore_signal(barrier, inc=1, device_id={"conf": peer, "state": y}, device_id_type=MESH)

    sent = []

    def send(src, dst, conf, state):
        n = len(sent)
        copy = pltpu.make_async_remote_copy(
            src_ref=src, dst_ref=dst, send_sem=send_sem.at[n], recv_sem=recv_sem.at[n],
            device_id={"conf": conf, "state": state}, device_id_type=MESH,
        )
        copy.start()
        sent.append(copy)
        return copy

    small[0].wait()
    small[1].wait()
    log_samples[...] = jnp.log(samples[...].astype(F32))
    for j in range(GROUP):
        cols = pl.ds(128 * j, 128)
        lifted[:, cols] = lifted[:, cols] + log_samples[j : j + 1, :]

    free_copies = None
    for it in range(ITERS):
        last = it == ITERS - 1
        top_me = jnp.max(lifted[...], axis=1, keepdims=True)
        mine[...] = jnp.broadcast_to(top_me, (B, 128))
        ext[it, 0] = pack(top_me)
        n_ext = 1
        if it > 0:
            first = jnp.where(y == 0, val_got[it - 1, 0, :, 0:1], jnp.zeros((B, 1), F32))
            ext[it, 1] = pack(first)
            n_ext = 2
        high, low = split(jnp.exp(lifted[...] - top_me))
        lhs[0:B, :] = high
        lhs[B : 2 * B, :] = low
        if it == 0:
            pl.semaphore_wait(barrier, 3 + GROUP - 1 + RING - 1)
        ext_copies = [send(ext.at[it, pl.ds(0, n_ext)], ext_got.at[it, k, pl.ds(0, n_ext)], c, peers[k]) for k in range(3)]

        row_copies = []
        phase1 = []
        for p in range(PIECES):
            if it == 0:
                for h in range(W // LW):
                    i = p * (W // LW) + h
                    loads[i].wait()

                    def low_energy(r, acc):
                        return jnp.minimum(acc, jnp.min(e_buf[i, pl.ds(r * 64, 64), :].reshape(8, 8, LW), axis=0))

                    least = lax.fori_loop(0, KS // 64, low_energy, jnp.full((8, LW), jnp.inf, F32), unroll=4)
                    shift = -jnp.min(least, axis=0, keepdims=True)
                    rows[p, 0:1, h * LW : (h + 1) * LW] = shift
                    rows[p, 1:2, h * LW : (h + 1) * LW] = jnp.where(y == 0, e_buf[i, 0:1, :], jnp.zeros((1, LW), F32))
                row_copies.append([send(rows.at[p], rows_got.at[k, p], c, peers[k]) for k in range(3)])
                for h in range(W // LW):
                    i = p * (W // LW) + h
                    shift = rows[p, 0:1, h * LW : (h + 1) * LW]

                    def boltz(r, carry):
                        at = pl.ds(r * 32, 32)
                        high, low = split(jnp.exp(-e_buf[i, at, :] - shift))
                        bh[p, at, h * LW : (h + 1) * LW] = high
                        bl[p, at, h * LW : (h + 1) * LW] = low
                        return carry

                    lax.fori_loop(0, KS // 32, boltz, 0, unroll=4)
            both = jnp.dot(lhs[...], bh[p], preferred_element_type=F32)
            rest = jnp.dot(lhs[0:B, :], bl[p], preferred_element_type=F32)
            part1[it, p] = both[0:B] + (both[B : 2 * B] + rest)
            phase1.append(send(part1.at[it, p], got1.at[it, p], c, peers[p % 2]))

        for copy in ext_copies:
            copy.wait_recv()
        tops = [mine[:, 0:1]] + [unpack(ext_got[it, k, 0]) for k in range(3)]
        pairs = [jnp.maximum(tops[0], tops[1]), jnp.maximum(tops[0], tops[2])]
        others = [jnp.maximum(tops[2], tops[3]), jnp.maximum(tops[1], tops[3])]
        top = jnp.maximum(pairs[0], others[0])
        own1 = [jnp.exp(tops[0] - pairs[k]) for k in range(2)]
        its1 = [jnp.exp(tops[1 + k] - pairs[k]) for k in range(2)]
        own2 = [jnp.exp(pairs[k] - top) for k in range(2)]
        its2 = [jnp.exp(others[k] - top) for k in range(2)]
        if it > 0:
            anchor = unpack(ext[it, 1])
            for k in range(3):
                anchor = anchor + unpack(ext_got[it, k, 1])
        phase2 = []
        for p in range(PIECES):
            k = p % 2
            a, b = own1[k], its1[k]
            if it == 0:
                for copy in row_copies[p]:
                    copy.wait_recv()
            m0, m1 = rows[p, 0:1, :], rows_got[k, p, 0:1, :]
            m = jnp.maximum(m0, m1)
            a, b = a * jnp.exp(m0 - m), b * jnp.exp(m1 - m)
            phase1[p].wait_recv()
            part2[it, p] = part1[it, p] * a + got1[it, p] * b
            phase2.append(send(part2.at[it, p], got2.at[it, p], c, peers[1 - k]))
        if it == 0:
            small[2].wait()
        first_total = jnp.zeros((B, 1), F32)
        for p in range(PIECES):
            k = p % 2
            a, b = own2[k], its2[k]
            ms = [rows[p, 0:1, :]] + [rows_got[j, p, 0:1, :] for j in range(3)]
            pair = jnp.maximum(ms[0], ms[1 + k])
            other = jnp.maximum(ms[2 - k], ms[3])
            m = jnp.maximum(pair, other)
            a, b = a * jnp.exp(pair - m), b * jnp.exp(other - m)
            phase2[p].wait_recv()
            denom = part2[it, p] * a + got2[it, p] * b
            ratio = counts[:, p * W : (p + 1) * W].astype(F32) / denom
            if last:
                lw_ref[:, p * W : (p + 1) * W] = jnp.log(denom) + (top - anchor)
                e0 = rows[p, 1:2, :] + rows_got[0, p, 1:2, :] + rows_got[1, p, 1:2, :] + rows_got[2, p, 1:2, :]
                first_total = first_total + jnp.sum(ratio * jnp.exp(-e0 - m), axis=1, keepdims=True)
            high, low = split(ratio * jnp.exp(ms[0] - m))
            rhs[0:B, :] = high
            rhs[B : 2 * B, :] = low
            dims = (((1,), (1,)), ((), ()))
            both = lax.dot_general(rhs[...], bh[p], dims, preferred_element_type=F32)
            rest = lax.dot_general(rhs[0:B, :], bl[p], dims, preferred_element_type=F32)
            terms = both[0:B] + (both[B : 2 * B] + rest)
            total[...] = terms if p == 0 else total[...] + terms

        height = B + 8 if last else B
        packed = pack(first_total) if last else None
        for j in range(GROUP):
            tot[it, j, 0:B, :] = total[:, 128 * j : 128 * (j + 1)]
            if last:
                tot[it, j, B : B + 8, :] = packed
        span = pl.ds(0, height)
        scatter = []
        for o in range(1, GROUP):
            to = (g + o) % GROUP
            scatter.append(send(tot.at[it, to, span], tot_got.at[it, o, span], z * GROUP + to, y))
        acc = tot[it, g, 0:height, :]
        for o in range(1, GROUP):
            scatter[o - 1].wait_recv()
            acc = acc + tot_got[it, o, 0:height, :]
        ring[it, 0:height, :] = acc
        ring_got[it, z, 0:height, :] = acc
        around = []
        for o in range(1, RING):
            around.append(send(ring.at[it, span], ring_got.at[it, z, span], ((z + o) % RING) * GROUP + g, y))
        for copy in around:
            copy.wait_recv()
        acc = ring_got[it, 0, 0:height, :]
        for k in range(1, RING):
            acc = acc + ring_got[it, k, 0:height, :]
        if last:
            value = jnp.log(unpack(acc[B : B + 8])) - jnp.log(acc[0:B])
        else:
            value = top - jnp.log(acc)
        val[it] = value
        val_got[it, g] = value
        gather = []
        for o in range(1, GROUP):
            to = (g + o) % GROUP
            gather.append(send(val.at[it], val_got.at[it, g], z * GROUP + to, y))
        for copy in gather:
            copy.wait_recv()
        for j in range(GROUP):
            cols = pl.ds(128 * j, 128)
            if last:
                free_ref[:, cols] = val_got[it, j]
            else:
                lifted[:, cols] = val_got[it, j] + log_samples[j : j + 1, :]
    for copy in sent:
        copy.wait_send()


def per_device(energies, samples, counts, initial):
    anywhere = pl.BlockSpec(memory_space=pl.ANY)
    inside = pl.BlockSpec(memory_space=pltpu.VMEM)
    copies = 3 * PIECES + ITERS * (3 + 2 * PIECES + 2 * (GROUP - 1) + RING - 1)
    vmem = pltpu.VMEM
    return pl.pallas_call(
        kernel,
        out_shape=(jax.ShapeDtypeStruct((B, KS), F32), jax.ShapeDtypeStruct((B, NS), F32)),
        in_specs=[anywhere] * 4,
        out_specs=(inside, inside),
        scratch_shapes=[
            vmem((LOADS, KS, LW), F32),
            vmem((PIECES, KS, W), BF16),
            vmem((PIECES, KS, W), BF16),
            vmem((GROUP, 128), jnp.int32),
            vmem((B, NS), jnp.int32),
            vmem((B, KS), F32),
            vmem((2 * B, KS), BF16),
            vmem((2 * B, W), BF16),
            vmem((B, KS), F32),
            vmem((B, 128), F32),
            vmem((GROUP, 128), F32),
            vmem((ITERS, PIECES, B, W), F32),
            vmem((ITERS, PIECES, B, W), F32),
            vmem((ITERS, PIECES, B, W), F32),
            vmem((ITERS, PIECES, B, W), F32),
            vmem((ITERS, 2, 8, 128), F32),
            vmem((ITERS, 3, 2, 8, 128), F32),
            vmem((PIECES, 2, W), F32),
            vmem((3, PIECES, 2, W), F32),
            vmem((ITERS, GROUP, B + 8, 128), F32),
            vmem((ITERS, GROUP, B + 8, 128), F32),
            vmem((ITERS, B + 8, 128), F32),
            vmem((ITERS, RING, B + 8, 128), F32),
            vmem((ITERS, B, 128), F32),
            vmem((ITERS, GROUP, B, 128), F32),
            pltpu.SemaphoreType.DMA((LOADS,)),
            pltpu.SemaphoreType.DMA((3,)),
            pltpu.SemaphoreType.DMA((copies,)),
            pltpu.SemaphoreType.DMA((copies,)),
        ],
        compiler_params=pltpu.CompilerParams(
            collective_id=0, has_side_effects=True, vmem_limit_bytes=56 * 2**20
        ),
    )(energies, samples.reshape(GROUP, 128), counts, initial)


def solution(mesh):
    in_specs = (P("state", "conf"), P("state"), P(None, "conf"), P(None, "state"))
    out_specs = (P(None, "state"), P(None, "conf"))
    return jax.shard_map(
        per_device, mesh=mesh, in_specs=in_specs, out_specs=out_specs, check_vma=False
    )
```

```python
import functools

import jax
import jax.numpy as jnp
from jax import lax
from jax.experimental import pallas as pl
from jax.experimental.pallas import tpu as pltpu
from jax.sharding import PartitionSpec as P

MESH = pl.DeviceIdType.MESH
ITERS = 2
B = 32
KS = 1024
NS = 2048
PIECES = 8
W = NS // PIECES
BATCH = 4
GROUP = 8
RING = 8
F32 = jnp.float32
BF16 = jnp.bfloat16


def diagonal(offset):
    return lax.broadcasted_iota(jnp.int32, (B, 128), 1) == lax.broadcasted_iota(jnp.int32, (B, 128), 0) + offset


def to_row(column, offset=0):
    return jnp.sum(jnp.where(diagonal(offset), column, 0.0), axis=0, keepdims=True)


def to_column(row, offset=0):
    return jnp.sum(jnp.where(diagonal(offset), row, 0.0), axis=1, keepdims=True)


def split(x):
    high = x.astype(BF16)
    low = (x - high.astype(F32)).astype(BF16)
    return high, low


def kernel(
    e_hbm, samples_hbm, counts_hbm, initial_hbm, free_ref, lw_ref,
    e_buf, bh, bl, samples, counts, lifted, lhs, rhs, mine, log_samples,
    part1, part2, got1, got2, ext, ext_got, rows, rows_got, tot, tot_got, ring, ring_got, val, val_got,
    load_sem, small_sem, send_sem, recv_sem,
):
    c = lax.axis_index("conf")
    y = lax.axis_index("state")
    z, g = c // GROUP, c % GROUP
    peers = (y + 1 - 2 * (y % 2), 3 - y, (y + 2) % 4)

    barrier = pltpu.get_barrier_semaphore()
    for peer in peers:
        pl.semaphore_signal(barrier, inc=1, device_id={"conf": c, "state": peer}, device_id_type=MESH)
    for o in range(1, GROUP):
        peer = z * GROUP + (g + o) % GROUP
        pl.semaphore_signal(barrier, inc=1, device_id={"conf": peer, "state": y}, device_id_type=MESH)
    for o in range(1, RING):
        peer = ((z + o) % RING) * GROUP + g
        pl.semaphore_signal(barrier, inc=1, device_id={"conf": peer, "state": y}, device_id_type=MESH)

    loads = []
    small = [
        pltpu.make_async_copy(samples_hbm, samples, small_sem.at[0]),
        pltpu.make_async_copy(initial_hbm, lifted, small_sem.at[1]),
        pltpu.make_async_copy(counts_hbm, counts, small_sem.at[2]),
    ]
    small[0].start()
    small[1].start()
    for i in range(PIECES):
        copy = pltpu.make_async_copy(e_hbm.at[:, pl.ds(i * W, W)], e_buf.at[i], load_sem.at[i])
        copy.start()
        loads.append(copy)
    small[2].start()

    sent = []

    def send(src, dst, conf, state):
        n = len(sent)
        copy = pltpu.make_async_remote_copy(
            src_ref=src, dst_ref=dst, send_sem=send_sem.at[n], recv_sem=recv_sem.at[n],
            device_id={"conf": conf, "state": state}, device_id_type=MESH,
        )
        copy.start()
        sent.append(copy)
        return copy

    drained = [0]

    def drain():
        for copy in sent[drained[0] :]:
            copy.wait_send()
        drained[0] = len(sent)

    small[0].wait()
    small[1].wait()
    log_samples[...] = jnp.log(samples[...].astype(F32))
    for j in range(GROUP):
        cols = pl.ds(128 * j, 128)
        lifted[:, cols] = lifted[:, cols] + log_samples[j : j + 1, :]

    free_copies = None
    for it in range(ITERS):
        last = it == ITERS - 1
        top_me = jnp.max(lifted[...], axis=1, keepdims=True)
        mine[...] = jnp.broadcast_to(top_me, (B, 128))
        line = to_row(top_me)
        if it > 0:
            line = line + to_row(jnp.where(y == 0, val_got[it - 1, 0, :, 0:1], jnp.zeros((B, 1), F32)), B)
        ext[it] = line
        high, low = split(jnp.exp(lifted[...] - top_me))
        lhs[0:B, :] = high
        lhs[B : 2 * B, :] = low
        row_copies = []
        phase1 = []
        if it == 0:
            pl.semaphore_wait(barrier, 3 + GROUP - 1 + RING - 1)
        ext_copies = [send(ext.at[it], ext_got.at[it, k], c, peers[k]) for k in (2, 0, 1)]
        for p in range(PIECES):
            if it == 0:
                loads[p].wait()

                def low_energy(r, acc):
                    return jnp.minimum(acc, jnp.min(e_buf[p, pl.ds(r * 64, 64), :].reshape(8, 8, W), axis=0))

                least = lax.fori_loop(0, KS // 64, low_energy, jnp.full((8, W), jnp.inf, F32), unroll=4)
                shift = -jnp.min(least, axis=0, keepdims=True)
                q, cols = p // BATCH, slice(p % BATCH * W, (p % BATCH + 1) * W)
                rows[q, 0:1, cols] = shift
                rows[q, 1:2, cols] = jnp.where(y == 0, e_buf[p, 0:1, :], jnp.zeros((1, W), F32))
                if p % BATCH == BATCH - 1:
                    row_copies.append([send(rows.at[q], rows_got.at[k, q], c, peers[k]) for k in (2, 0, 1)])

                def boltz(r, carry):
                    at = pl.ds(r * 32, 32)
                    high, low = split(jnp.exp(-e_buf[p, at, :] - shift))
                    bh[p, at, :] = high
                    bl[p, at, :] = low
                    return carry

                lax.fori_loop(0, KS // 32, boltz, 0, unroll=4)
            both = jnp.dot(lhs[...], bh[p], preferred_element_type=F32)
            rest = jnp.dot(lhs[0:B, :], bl[p], preferred_element_type=F32)
            part1[it, p] = both[0:B] + (both[B : 2 * B] + rest)
            phase1.append(send(part1.at[it, p], got1.at[it, p], c, peers[p % 2]))

        for copy in ext_copies:
            copy.wait_recv()
        tops = [mine[:, 0:1]] + [to_column(ext_got[it, k]) for k in range(3)]
        pairs = [jnp.maximum(tops[0], tops[1]), jnp.maximum(tops[0], tops[2])]
        others = [jnp.maximum(tops[2], tops[3]), jnp.maximum(tops[1], tops[3])]
        top = jnp.maximum(pairs[0], others[0])
        own1 = [jnp.exp(tops[0] - pairs[k]) for k in range(2)]
        its1 = [jnp.exp(tops[1 + k] - pairs[k]) for k in range(2)]
        own2 = [jnp.exp(pairs[k] - top) for k in range(2)]
        its2 = [jnp.exp(others[k] - top) for k in range(2)]
        if it > 0:
            line = ext[it] + (ext_got[it, 0] + (ext_got[it, 1] + ext_got[it, 2]))
            anchor = to_column(line, B)
        phase2 = []
        for p in range(PIECES):
            k = p % 2
            a, b = own1[k], its1[k]
            q, cols = p // BATCH, slice(p % BATCH * W, (p % BATCH + 1) * W)
            if it == 0 and p % BATCH == 0:
                for copy in row_copies[q]:
                    copy.wait_recv()
            m0, m1 = rows[q, 0:1, cols], rows_got[k, q, 0:1, cols]
            m = jnp.maximum(m0, m1)
            a, b = a * jnp.exp(m0 - m), b * jnp.exp(m1 - m)
            phase1[p].wait_recv()
            part2[it, p] = part1[it, p] * a + got1[it, p] * b
            phase2.append(send(part2.at[it, p], got2.at[it, p], c, peers[1 - k]))
        if it == 0:
            small[2].wait()
        first_total = jnp.zeros((B, 128), F32)
        for p in range(PIECES):
            k = p % 2
            a, b = own2[k], its2[k]
            q, cols = p // BATCH, slice(p % BATCH * W, (p % BATCH + 1) * W)
            ms = [rows[q, 0:1, cols]] + [rows_got[j, q, 0:1, cols] for j in range(3)]
            pair = jnp.maximum(ms[0], ms[1 + k])
            other = jnp.maximum(ms[2 - k], ms[3])
            m = jnp.maximum(pair, other)
            a, b = a * jnp.exp(pair - m), b * jnp.exp(other - m)
            if last:
                e0 = rows[q, 1:2, cols] + rows_got[0, q, 1:2, cols] + rows_got[1, q, 1:2, cols] + rows_got[2, q, 1:2, cols]
                first_boltz = jnp.exp(-e0 - m)
            phase2[p].wait_recv()
            denom = part2[it, p] * a + got2[it, p] * b
            ratio = counts[:, p * W : (p + 1) * W].astype(F32) / denom
            if last:
                lw_ref[:, p * W : (p + 1) * W] = denom
                first_terms = ratio * first_boltz
                first_total = first_total + (first_terms[:, :128] + first_terms[:, 128:])
            high, low = split(ratio * jnp.exp(ms[0] - m))
            rhs[0:B, :] = high
            rhs[B : 2 * B, :] = low
            dims = (((1,), (1,)), ((), ()))
            if p < PIECES - 1:
                both = lax.dot_general(rhs[...], bh[p], dims, preferred_element_type=F32)
                rest = lax.dot_general(rhs[0:B, :], bl[p], dims, preferred_element_type=F32)
                terms = both[0:B] + (both[B : 2 * B] + rest)
                for j in range(GROUP):
                    part = terms[:, 128 * j : 128 * (j + 1)]
                    tot[it, j, 0:B, :] = part if p == 0 else tot[it, j, 0:B, :] + part

        height = B + 1 if last else B
        span = pl.ds(0, height)
        if last:
            first_line = to_row(jnp.sum(first_total, axis=1, keepdims=True))
            for j in range(GROUP):
                tot[it, j, B : B + 1, :] = first_line
        scatter = []
        p = PIECES - 1
        for ox in (2, 1, 3, 0):
            x = (g // 2 + ox) % (GROUP // 2)
            at = pl.ds(pl.multiple_of(x * 256, 256), 256)
            both = lax.dot_general(rhs[...], bh[p, at, :], dims, preferred_element_type=F32)
            rest = lax.dot_general(rhs[0:B, :], bl[p, at, :], dims, preferred_element_type=F32)
            terms = both[0:B] + (both[B : 2 * B] + rest)
            for core in range(2):
                j = 2 * x + core
                tot[it, j, 0:B, :] = tot[it, j, 0:B, :] + terms[:, 128 * core : 128 * (core + 1)]
            for oc in (0, 1):
                if ox == 0 and oc == 0:
                    continue
                slot = 2 * ox + oc
                to = 2 * x + (g + oc) % 2
                scatter.append((slot, send(tot.at[it, to, span], tot_got.at[it, slot, span], z * GROUP + to, y)))
        if it == 0:
            drain()
        acc = tot[it, g, 0:height, :]
        for slot, copy in scatter[::-1]:
            copy.wait_recv()
            acc = acc + tot_got[it, slot, 0:height, :]
        ring[it, 0:height, :] = acc
        around = []
        for o in (4, 3, 5, 2, 6, 1, 7):
            around.append(send(ring.at[it, span], ring_got.at[it, z, span], ((z + o) % RING) * GROUP + g, y))
        ring_got[it, z, 0:height, :] = acc
        drain()
        if last:
            for p in range(PIECES):
                cols = pl.ds(p * W, W)
                lw_ref[:, cols] = jnp.log(lw_ref[:, cols]) + (top - anchor)
        for copy in around:
            copy.wait_recv()
        acc = ring_got[it, 0, 0:height, :]
        for k in range(1, RING):
            acc = acc + ring_got[it, k, 0:height, :]
        if last:
            value = jnp.log(to_column(acc[B : B + 1])) - jnp.log(acc[0:B])
        else:
            value = top - jnp.log(acc)
        val[it] = value
        gather = []
        for ox, oc in ((2, 0), (2, 1), (1, 0), (1, 1), (3, 0), (3, 1), (0, 1)):
            to = 2 * ((g // 2 + ox) % (GROUP // 2)) + (g + oc) % 2
            gather.append(send(val.at[it], val_got.at[it, g], z * GROUP + to, y))
        val_got[it, g] = value
        for copy in gather:
            copy.wait_recv()
        for j in range(GROUP):
            cols = pl.ds(128 * j, 128)
            if last:
                free_ref[:, cols] = val_got[it, j]
            else:
                lifted[:, cols] = val_got[it, j] + log_samples[j : j + 1, :]
    drain()


def finish(free_in, lw_in, free_out, lw_out):
    free_out[...] = free_in[...]
    lw_out[...] = lw_in[...]


def per_device(energies, samples, counts, initial):
    outside = pl.BlockSpec(memory_space=pl.ANY)
    inside = pl.BlockSpec(memory_space=pltpu.VMEM)
    copies = 3 * PIECES // BATCH + ITERS * (3 + 2 * PIECES + 2 * (GROUP - 1) + RING - 1)
    vmem = pltpu.VMEM
    free, log_weight = pl.pallas_call(
        kernel,
        out_shape=tuple(jax.ShapeDtypeStruct((B, n), F32) for n in (KS, NS)),
        in_specs=[outside] * 4,
        out_specs=(inside,) * 2,
        scratch_shapes=[
            vmem((PIECES, KS, W), F32),
            vmem((PIECES, KS, W), BF16),
            vmem((PIECES, KS, W), BF16),
            vmem((GROUP, 128), jnp.int32),
            vmem((B, NS), jnp.int32),
            vmem((B, KS), F32),
            vmem((2 * B, KS), BF16),
            vmem((2 * B, W), BF16),
            vmem((B, 128), F32),
            vmem((GROUP, 128), F32),
            vmem((ITERS, PIECES, B, W), F32),
            vmem((ITERS, PIECES, B, W), F32),
            vmem((ITERS, PIECES, B, W), F32),
            vmem((ITERS, PIECES, B, W), F32),
            vmem((ITERS, 1, 128), F32),
            vmem((ITERS, 3, 1, 128), F32),
            vmem((PIECES // BATCH, 2, BATCH * W), F32),
            vmem((3, PIECES // BATCH, 2, BATCH * W), F32),
            vmem((ITERS, GROUP, B + 8, 128), F32),
            vmem((ITERS, GROUP, B + 8, 128), F32),
            vmem((ITERS, B + 8, 128), F32),
            vmem((ITERS, RING, B + 8, 128), F32),
            vmem((ITERS, B, 128), F32),
            vmem((ITERS, GROUP, B, 128), F32),
            pltpu.SemaphoreType.DMA((PIECES,)),
            pltpu.SemaphoreType.DMA((3,)),
            pltpu.SemaphoreType.DMA((copies,)),
            pltpu.SemaphoreType.DMA((copies,)),
        ],
        compiler_params=pltpu.CompilerParams(
            collective_id=0, has_side_effects=True, vmem_limit_bytes=56 * 2**20
        ),
    )(energies, samples.reshape(GROUP, 128), counts, initial)
    return pl.pallas_call(
        finish,
        out_shape=(jax.ShapeDtypeStruct((B, KS), F32), jax.ShapeDtypeStruct((B, NS), F32)),
        in_specs=[inside] * 2,
        out_specs=(inside,) * 2,
    )(free, log_weight)


def solution(mesh):
    in_specs = (P("state", "conf"), P("state"), P(None, "conf"), P(None, "state"))
    out_specs = (P(None, "state"), P(None, "conf"))
    return jax.shard_map(
        per_device, mesh=mesh, in_specs=in_specs, out_specs=out_specs, check_vma=False
    )
```

```python
import functools

import jax
import jax.numpy as jnp
from jax import lax
from jax.experimental import pallas as pl
from jax.experimental.pallas import tpu as pltpu
from jax.sharding import PartitionSpec as P

MESH = pl.DeviceIdType.MESH
ITERS = 2
B = 32
KS = 1024
NS = 2048
PIECES = 8
W = NS // PIECES
PAIRS = PIECES // 2
DEEP = 256
GROUP = 8
RING = 8
F32 = jnp.float32
BF16 = jnp.bfloat16


def diagonal(offset):
    return lax.broadcasted_iota(jnp.int32, (B, 128), 1) == lax.broadcasted_iota(jnp.int32, (B, 128), 0) + offset


def to_row(column, offset=0):
    return jnp.sum(jnp.where(diagonal(offset), column, 0.0), axis=0, keepdims=True)


def to_column(row, offset=0):
    return jnp.sum(jnp.where(diagonal(offset), row, 0.0), axis=1, keepdims=True)


def split(x):
    high = x.astype(BF16)
    low = (x - high.astype(F32)).astype(BF16)
    return high, low


def kernel(
    e_hbm, samples_hbm, counts_hbm, initial_hbm, free_ref, lw_ref,
    e_buf, bh, bl, samples, counts, lifted, lhs, rhs, mine, log_samples,
    part1, part2, got1, got2, ext, ext_got, rows, rows_got, tot, tot_got, ring, ring_got, val, val_got,
    load_sem, small_sem, send_sem, recv_sem,
):
    c = lax.axis_index("conf")
    y = lax.axis_index("state")
    z, g = c // GROUP, c % GROUP
    peers = (y + 1 - 2 * (y % 2), 3 - y, (y + 2) % 4)

    barrier = pltpu.get_barrier_semaphore()
    for peer in peers:
        pl.semaphore_signal(barrier, inc=1, device_id={"conf": c, "state": peer}, device_id_type=MESH)
    for o in range(1, GROUP):
        peer = z * GROUP + (g + o) % GROUP
        pl.semaphore_signal(barrier, inc=1, device_id={"conf": peer, "state": y}, device_id_type=MESH)
    for o in range(1, RING):
        peer = ((z + o) % RING) * GROUP + g
        pl.semaphore_signal(barrier, inc=1, device_id={"conf": peer, "state": y}, device_id_type=MESH)

    small = [
        pltpu.make_async_copy(samples_hbm, samples, small_sem.at[0]),
        pltpu.make_async_copy(initial_hbm, lifted, small_sem.at[1]),
        pltpu.make_async_copy(counts_hbm, counts, small_sem.at[2]),
    ]
    small[0].start()
    small[1].start()
    loads = [pltpu.make_async_copy(e_hbm.at[:, pl.ds(p * W, W)], e_buf.at[p], load_sem.at[p]) for p in range(PIECES)]
    for copy in loads:
        copy.start()
    small[2].start()

    def remote(src, dst, conf, state, n):
        return pltpu.make_async_remote_copy(
            src_ref=src, dst_ref=dst, send_sem=send_sem.at[n], recv_sem=recv_sem.at[n],
            device_id={"conf": conf, "state": state}, device_id_type=MESH,
        )

    used = [0]

    def take(n):
        used[0] += n
        return used[0] - n

    undrained = []

    def send(src, dst, conf, state):
        copy = remote(src, dst, conf, state, take(1))
        copy.start()
        undrained.append(copy.wait_send)
        return copy

    def drain():
        for wait in undrained:
            wait()
        undrained.clear()

    def row_copies(t, k):
        return remote(rows.at[t], rows_got.at[k, t], c, peers[k], row_base + 3 * t + k)

    def wait_rows():
        @pl.loop(0, PAIRS)
        def _(t):
            for k in range(3):
                row_copies(t, k).wait_send()

    row_base = take(3 * PAIRS)

    small[0].wait()
    small[1].wait()
    log_samples[...] = jnp.log(samples[...].astype(F32))
    for j in range(GROUP):
        cols = pl.ds(128 * j, 128)
        lifted[:, cols] = lifted[:, cols] + log_samples[j : j + 1, :]

    for it in range(ITERS):
        last = it == ITERS - 1
        top_me = jnp.max(lifted[...], axis=1, keepdims=True)
        mine[...] = jnp.broadcast_to(top_me, (B, 128))
        high, low = split(jnp.exp(lifted[...] - top_me))
        lhs[0:B, :] = high
        lhs[B : 2 * B, :] = low
        line = to_row(top_me)
        if it > 0:
            line = line + to_row(jnp.where(y == 0, val_got[it - 1, 0, :, 0:1], jnp.zeros((B, 1), F32)), B)
        ext[it] = line
        if it == 0:
            pl.semaphore_wait(barrier, 3 + GROUP - 1 + RING - 1)
        ext_copies = [send(ext.at[it], ext_got.at[it, k], c, peers[k]) for k in (2, 0, 1)]
        base1, base2 = take(PIECES), take(PIECES)

        def copy1(p, k):
            return remote(part1.at[it, p], got1.at[it, p], c, peers[k], base1 + p)

        def copy2(p, k):
            return remote(part2.at[it, p], got2.at[it, p], c, peers[1 - k], base2 + p)

        def wait_parts():
            @pl.loop(0, PAIRS)
            def _(t):
                for k in range(2):
                    copy1(2 * t + k, k).wait_send()
                    copy2(2 * t + k, k).wait_send()

        @pl.loop(0, PAIRS)
        def _(t):
            leasts = []
            if it == 0:
                for k in range(2):
                    p = 2 * t + k
                    pltpu.make_async_copy(e_hbm.at[:, pl.ds(0, W)], e_buf.at[p], load_sem.at[p]).wait()

                    def low_energy(r, acc):
                        return jnp.minimum(acc, jnp.min(e_buf[p, pl.ds(r * 64, 64), :].reshape(8, 8, W), axis=0))

                    least = lax.fori_loop(0, KS // 64, low_energy, jnp.full((8, W), jnp.inf, F32), unroll=16)
                    least = jnp.min(least, axis=0, keepdims=True)
                    cols = slice(k * W, (k + 1) * W)
                    rows[t, 0:1, cols] = -least
                    rows[t, 1:2, cols] = jnp.where(y == 0, e_buf[p, 0:1, :], jnp.zeros((1, W), F32))
                    leasts.append(least)
                for k in (2, 0, 1):
                    row_copies(t, k).start()
            for k in range(2):
                p = 2 * t + k
                if it == 0:
                    acc = jnp.zeros((B, W), F32)
                    for d in range(KS // DEEP):
                        for r in range(d * DEEP, (d + 1) * DEEP, 32):
                            high, low = split(jnp.exp(leasts[k] - e_buf[p, r : r + 32, :]))
                            bh[p, r : r + 32, :] = high
                            bl[p, r : r + 32, :] = low
                        at = slice(d * DEEP, (d + 1) * DEEP)
                        both = jnp.dot(lhs[:, at], bh[p, at, :], preferred_element_type=F32)
                        rest = jnp.dot(lhs[0:B, at], bl[p, at, :], preferred_element_type=F32)
                        acc = acc + (both[0:B] + (both[B : 2 * B] + rest))
                    part1[it, p] = acc
                else:
                    both = jnp.dot(lhs[...], bh[p], preferred_element_type=F32)
                    rest = jnp.dot(lhs[0:B, :], bl[p], preferred_element_type=F32)
                    part1[it, p] = both[0:B] + (both[B : 2 * B] + rest)
                copy1(p, k).start()

        for copy in ext_copies:
            copy.wait_recv()
        tops = [mine[:, 0:1]] + [to_column(ext_got[it, k]) for k in range(3)]
        pairs = [jnp.maximum(tops[0], tops[1]), jnp.maximum(tops[0], tops[2])]
        others = [jnp.maximum(tops[2], tops[3]), jnp.maximum(tops[1], tops[3])]
        top = jnp.maximum(pairs[0], others[0])
        own1 = [jnp.exp(tops[0] - pairs[k]) for k in range(2)]
        its1 = [jnp.exp(tops[1 + k] - pairs[k]) for k in range(2)]
        own2 = [jnp.exp(pairs[k] - top) for k in range(2)]
        its2 = [jnp.exp(others[k] - top) for k in range(2)]
        if it > 0:
            line = ext[it] + (ext_got[it, 0] + (ext_got[it, 1] + ext_got[it, 2]))
            anchor = to_column(line, B)

        @pl.loop(0, PAIRS)
        def _(t):
            if it == 0:
                for k in range(3):
                    row_copies(t, k).wait_recv()
            for k in range(2):
                p = 2 * t + k
                cols = slice(k * W, (k + 1) * W)
                m0, m1 = rows[t, 0:1, cols], rows_got[k, t, 0:1, cols]
                m = jnp.maximum(m0, m1)
                a, b = own1[k] * jnp.exp(m0 - m), its1[k] * jnp.exp(m1 - m)
                copy1(p, k).wait_recv()
                part2[it, p] = part1[it, p] * a + got1[it, p] * b
                copy2(p, k).start()

        tot[it] = jnp.zeros((GROUP, B + 8, 128), F32)
        if it == 0:
            small[2].wait()
        dims = (((1,), (1,)), ((), ()))

        def ratios(t, k, first_total):
            p = 2 * t + k
            cols = slice(k * W, (k + 1) * W)
            ms = [rows[t, 0:1, cols]] + [rows_got[j, t, 0:1, cols] for j in range(3)]
            pair = jnp.maximum(ms[0], ms[1 + k])
            other = jnp.maximum(ms[2 - k], ms[3])
            m = jnp.maximum(pair, other)
            a, b = own2[k] * jnp.exp(pair - m), its2[k] * jnp.exp(other - m)
            own_scale = jnp.exp(ms[0] - m)
            whole = pl.ds(pl.multiple_of(p * W, W), W)
            weight = counts[:, whole].astype(F32)
            if last:
                e0 = rows[t, 1:2, cols] + rows_got[0, t, 1:2, cols] + rows_got[1, t, 1:2, cols] + rows_got[2, t, 1:2, cols]
                first_boltz = jnp.exp(-e0 - m)
            copy2(p, k).wait_recv()
            denom = part2[it, p] * a + got2[it, p] * b
            ratio = weight / denom
            high, low = split(ratio * own_scale)
            rhs[k, 0:B, :] = high
            rhs[k, B : 2 * B, :] = low
            if last:
                lw_ref[:, whole] = denom
                first_terms = ratio * first_boltz
                first_total = first_total + (first_terms[:, :128] + first_terms[:, 128:])
            return first_total

        def terms(p, k, x):
            at = pl.ds(pl.multiple_of(x * 256, 256), 256)
            both = lax.dot_general(rhs[k], bh[p, at, :], dims, preferred_element_type=F32)
            rest = lax.dot_general(rhs[k, 0:B, :], bl[p, at, :], dims, preferred_element_type=F32)
            made = both[0:B] + (both[B : 2 * B] + rest)
            for core in range(2):
                j = 2 * x + core
                tot[it, j, 0:B, :] = tot[it, j, 0:B, :] + made[:, 128 * core : 128 * (core + 1)]

        def both_pieces(t, first_total):
            for k in range(2):
                first_total = ratios(t, k, first_total)
                for x in range(GROUP // 2):
                    terms(2 * t + k, k, x)
            return first_total

        first_total = lax.fori_loop(0, PAIRS - 1, both_pieces, jnp.zeros((B, 128), F32))
        first_total = ratios(PAIRS - 1, 0, first_total)
        for x in range(GROUP // 2):
            terms(PIECES - 2, 0, x)
        first_total = ratios(PAIRS - 1, 1, first_total)

        height = B + 1 if last else B
        span = pl.ds(0, height)
        if last:
            first_line = to_row(jnp.sum(first_total, axis=1, keepdims=True))
            for j in range(GROUP):
                tot[it, j, B : B + 1, :] = first_line
        scatter = []
        for ox in (2, 1, 3, 0):
            x = (g // 2 + ox) % (GROUP // 2)
            terms(PIECES - 1, 1, x)
            for oc in (0, 1):
                if ox == 0 and oc == 0:
                    continue
                slot = 2 * ox + oc
                to = 2 * x + (g + oc) % 2
                scatter.append((slot, send(tot.at[it, to, span], tot_got.at[it, slot, span], z * GROUP + to, y)))
        if it == 0:
            wait_rows()
        wait_parts()
        acc = tot[it, g, 0:height, :]
        for slot, copy in scatter[::-1]:
            copy.wait_recv()
            acc = acc + tot_got[it, slot, 0:height, :]
        ring[it, 0:height, :] = acc
        around = []
        for o in (4, 3, 5, 2, 6, 1, 7):
            around.append(send(ring.at[it, span], ring_got.at[it, z, span], ((z + o) % RING) * GROUP + g, y))
        ring_got[it, z, 0:height, :] = acc
        drain()
        if last:

            @pl.loop(0, PIECES)
            def _(p):
                whole = pl.ds(pl.multiple_of(p * W, W), W)
                lw_ref[:, whole] = jnp.log(lw_ref[:, whole]) + (top - anchor)

        for copy in around:
            copy.wait_recv()
        acc = ring_got[it, 0, 0:height, :]
        for k in range(1, RING):
            acc = acc + ring_got[it, k, 0:height, :]
        if last:
            value = jnp.log(to_column(acc[B : B + 1])) - jnp.log(acc[0:B])
        else:
            value = top - jnp.log(acc)
        val[it] = value
        gather = []
        for ox, oc in ((2, 0), (2, 1), (1, 0), (1, 1), (3, 0), (3, 1), (0, 1)):
            to = 2 * ((g // 2 + ox) % (GROUP // 2)) + (g + oc) % 2
            gather.append(send(val.at[it], val_got.at[it, g], z * GROUP + to, y))
        val_got[it, g] = value
        for copy in gather:
            copy.wait_recv()
        for j in range(GROUP):
            cols = pl.ds(128 * j, 128)
            if last:
                free_ref[:, cols] = val_got[it, j]
            else:
                lifted[:, cols] = val_got[it, j] + log_samples[j : j + 1, :]
    drain()


def finish(free_in, lw_in, free_out, lw_out):
    free_out[...] = free_in[...]
    lw_out[...] = lw_in[...]


def per_device(energies, samples, counts, initial):
    outside = pl.BlockSpec(memory_space=pl.ANY)
    inside = pl.BlockSpec(memory_space=pltpu.VMEM)
    copies = 3 * PAIRS + ITERS * (3 + 2 * PIECES + 2 * (GROUP - 1) + RING - 1)
    vmem = pltpu.VMEM
    free, log_weight = pl.pallas_call(
        kernel,
        out_shape=tuple(jax.ShapeDtypeStruct((B, n), F32) for n in (KS, NS)),
        in_specs=[outside] * 4,
        out_specs=(inside,) * 2,
        scratch_shapes=[
            vmem((PIECES, KS, W), F32),
            vmem((PIECES, KS, W), BF16),
            vmem((PIECES, KS, W), BF16),
            vmem((GROUP, 128), jnp.int32),
            vmem((B, NS), jnp.int32),
            vmem((B, KS), F32),
            vmem((2 * B, KS), BF16),
            vmem((2, 2 * B, W), BF16),
            vmem((B, 128), F32),
            vmem((GROUP, 128), F32),
            vmem((ITERS, PIECES, B, W), F32),
            vmem((ITERS, PIECES, B, W), F32),
            vmem((ITERS, PIECES, B, W), F32),
            vmem((ITERS, PIECES, B, W), F32),
            vmem((ITERS, 1, 128), F32),
            vmem((ITERS, 3, 1, 128), F32),
            vmem((PAIRS, 2, 2 * W), F32),
            vmem((3, PAIRS, 2, 2 * W), F32),
            vmem((ITERS, GROUP, B + 8, 128), F32),
            vmem((ITERS, GROUP, B + 8, 128), F32),
            vmem((ITERS, B + 8, 128), F32),
            vmem((ITERS, RING, B + 8, 128), F32),
            vmem((ITERS, B, 128), F32),
            vmem((ITERS, GROUP, B, 128), F32),
            pltpu.SemaphoreType.DMA((PIECES,)),
            pltpu.SemaphoreType.DMA((3,)),
            pltpu.SemaphoreType.DMA((copies,)),
            pltpu.SemaphoreType.DMA((copies,)),
        ],
        compiler_params=pltpu.CompilerParams(
            collective_id=0, has_side_effects=True, vmem_limit_bytes=56 * 2**20
        ),
    )(energies, samples.reshape(GROUP, 128), counts, initial)
    return pl.pallas_call(
        finish,
        out_shape=(jax.ShapeDtypeStruct((B, KS), F32), jax.ShapeDtypeStruct((B, NS), F32)),
        in_specs=[inside] * 2,
        out_specs=(inside,) * 2,
    )(free, log_weight)


def solution(mesh):
    in_specs = (P("state", "conf"), P("state"), P(None, "conf"), P(None, "state"))
    out_specs = (P(None, "state"), P(None, "conf"))
    return jax.shard_map(
        per_device, mesh=mesh, in_specs=in_specs, out_specs=out_specs, check_vma=False
    )
```

```python
import functools

import jax
import jax.numpy as jnp
from jax import lax
from jax.experimental import pallas as pl
from jax.experimental.pallas import tpu as pltpu
from jax.sharding import PartitionSpec as P

MESH = pl.DeviceIdType.MESH
ITERS = 2
B = 32
KS = 1024
NS = 2048
PIECES = 8
W = NS // PIECES
PAIRS = PIECES // 2
HELD = 1
DEEP = 256
GROUP = 8
RING = 8
F32 = jnp.float32
BF16 = jnp.bfloat16


def diagonal(offset):
    return lax.broadcasted_iota(jnp.int32, (B, 128), 1) == lax.broadcasted_iota(jnp.int32, (B, 128), 0) + offset


def to_row(column, offset=0):
    return jnp.sum(jnp.where(diagonal(offset), column, 0.0), axis=0, keepdims=True)


def to_column(row, offset=0):
    return jnp.sum(jnp.where(diagonal(offset), row, 0.0), axis=1, keepdims=True)


def split(x):
    high = x.astype(BF16)
    low = (x - high.astype(F32)).astype(BF16)
    return high, low


def kernel(
    e_hbm, samples_hbm, counts_hbm, initial_hbm, free_ref, lw_ref,
    e_buf, bh, bl, samples, counts, lifted, lhs, rhs, mine, log_samples,
    part1, part2, got1, got2, ext, ext_got, rows, rows_got, tot, tot_got, ring, ring_got, val, val_got,
    load_sem, small_sem, send_sem, recv_sem,
):
    c = lax.axis_index("conf")
    y = lax.axis_index("state")
    z, g = c // GROUP, c % GROUP
    peers = (y + 1 - 2 * (y % 2), 3 - y, (y + 2) % 4)

    barrier = pltpu.get_barrier_semaphore()
    for peer in peers:
        pl.semaphore_signal(barrier, inc=1, device_id={"conf": c, "state": peer}, device_id_type=MESH)
    for o in range(1, GROUP):
        peer = z * GROUP + (g + o) % GROUP
        pl.semaphore_signal(barrier, inc=1, device_id={"conf": peer, "state": y}, device_id_type=MESH)
    for o in range(1, RING):
        peer = ((z + o) % RING) * GROUP + g
        pl.semaphore_signal(barrier, inc=1, device_id={"conf": peer, "state": y}, device_id_type=MESH)

    small = [
        pltpu.make_async_copy(samples_hbm, samples, small_sem.at[0]),
        pltpu.make_async_copy(initial_hbm, lifted, small_sem.at[1]),
        pltpu.make_async_copy(counts_hbm, counts, small_sem.at[2]),
    ]
    small[0].start()
    small[1].start()
    loads = [pltpu.make_async_copy(e_hbm.at[:, pl.ds(p * W, W)], e_buf.at[p], load_sem.at[p]) for p in range(PIECES)]
    for copy in loads:
        copy.start()
    small[2].start()

    def remote(src, dst, conf, state, n):
        return pltpu.make_async_remote_copy(
            src_ref=src, dst_ref=dst, send_sem=send_sem.at[n], recv_sem=recv_sem.at[n],
            device_id={"conf": conf, "state": state}, device_id_type=MESH,
        )

    used = [0]

    def take(n):
        used[0] += n
        return used[0] - n

    undrained = []

    def send(src, dst, conf, state):
        copy = remote(src, dst, conf, state, take(1))
        copy.start()
        undrained.append(copy.wait_send)
        return copy

    def drain():
        for wait in undrained:
            wait()
        undrained.clear()

    def row_copies(t, k):
        return remote(rows.at[t], rows_got.at[k, t], c, peers[k], row_base + 3 * t + k)

    def wait_rows():
        @pl.loop(0, PAIRS)
        def _(t):
            for k in range(3):
                row_copies(t, k).wait_send()

    def send_rows(t):
        for k in (2, 0, 1):
            row_copies(t, k).start()

    row_base = take(3 * PAIRS)

    small[0].wait()
    small[1].wait()
    log_samples[...] = jnp.log(samples[...].astype(F32))
    for j in range(GROUP):
        cols = pl.ds(128 * j, 128)
        lifted[:, cols] = lifted[:, cols] + log_samples[j : j + 1, :]

    for it in range(ITERS):
        last = it == ITERS - 1
        top_me = jnp.max(lifted[...], axis=1, keepdims=True)
        mine[...] = jnp.broadcast_to(top_me, (B, 128))
        high, low = split(jnp.exp(lifted[...] - top_me))
        lhs[0:B, :] = high
        lhs[B : 2 * B, :] = low
        line = to_row(top_me)
        if it > 0:
            line = line + to_row(jnp.where(y == 0, val_got[it - 1, 0, :, 0:1], jnp.zeros((B, 1), F32)), B)
        ext[it] = line
        base1, base2 = take(PIECES), take(PIECES)

        def copy1(p, k):
            return remote(part1.at[it, p], got1.at[it, p], c, peers[k], base1 + p)

        def copy2(p, k):
            return remote(part2.at[it, p], got2.at[it, p], c, peers[1 - k], base2 + p)

        def wait_parts():
            @pl.loop(0, PAIRS)
            def _(t):
                for k in range(2):
                    copy1(2 * t + k, k).wait_send()
                    copy2(2 * t + k, k).wait_send()

        def products(t, sending):
            leasts = []
            if it == 0:
                for k in range(2):
                    p = 2 * t + k
                    pltpu.make_async_copy(e_hbm.at[:, pl.ds(0, W)], e_buf.at[p], load_sem.at[p]).wait()

                    def low_energy(r, acc):
                        return jnp.minimum(acc, jnp.min(e_buf[p, pl.ds(r * 64, 64), :].reshape(8, 8, W), axis=0))

                    least = lax.fori_loop(0, KS // 64, low_energy, jnp.full((8, W), jnp.inf, F32), unroll=16)
                    least = jnp.min(least, axis=0, keepdims=True)
                    cols = slice(k * W, (k + 1) * W)
                    rows[t, 0:1, cols] = -least
                    rows[t, 1:2, cols] = jnp.where(y == 0, e_buf[p, 0:1, :], jnp.zeros((1, W), F32))
                    leasts.append(least)
                if sending:
                    send_rows(t)
            for k in range(2):
                p = 2 * t + k
                if it == 0:
                    acc = jnp.zeros((B, W), F32)
                    for d in range(KS // DEEP):
                        for r in range(d * DEEP, (d + 1) * DEEP, 32):
                            high, low = split(jnp.exp(leasts[k] - e_buf[p, r : r + 32, :]))
                            bh[p, r : r + 32, :] = high
                            bl[p, r : r + 32, :] = low
                        at = slice(d * DEEP, (d + 1) * DEEP)
                        both = jnp.dot(lhs[:, at], bh[p, at, :], preferred_element_type=F32)
                        rest = jnp.dot(lhs[0:B, at], bl[p, at, :], preferred_element_type=F32)
                        acc = acc + (both[0:B] + (both[B : 2 * B] + rest))
                    part1[it, p] = acc
                else:
                    both = jnp.dot(lhs[...], bh[p], preferred_element_type=F32)
                    rest = jnp.dot(lhs[0:B, :], bl[p], preferred_element_type=F32)
                    part1[it, p] = both[0:B] + (both[B : 2 * B] + rest)
                if sending:
                    copy1(p, k).start()

        held = HELD if it == 0 else 0
        if held:

            @pl.loop(0, held)
            def _(t):
                products(t, False)

        if it == 0:
            pl.semaphore_wait(barrier, 3 + GROUP - 1 + RING - 1)
        ext_copies = [send(ext.at[it], ext_got.at[it, k], c, peers[k]) for k in (2, 0, 1)]
        if held:

            @pl.loop(0, held)
            def _(t):
                send_rows(t)
                for k in range(2):
                    copy1(2 * t + k, k).start()

        if held < PAIRS:

            @pl.loop(held, PAIRS)
            def _(t):
                products(t, True)

        for copy in ext_copies:
            copy.wait_recv()
        tops = [mine[:, 0:1]] + [to_column(ext_got[it, k]) for k in range(3)]
        pairs = [jnp.maximum(tops[0], tops[1]), jnp.maximum(tops[0], tops[2])]
        others = [jnp.maximum(tops[2], tops[3]), jnp.maximum(tops[1], tops[3])]
        top = jnp.maximum(pairs[0], others[0])
        own1 = [jnp.exp(tops[0] - pairs[k]) for k in range(2)]
        its1 = [jnp.exp(tops[1 + k] - pairs[k]) for k in range(2)]
        own2 = [jnp.exp(pairs[k] - top) for k in range(2)]
        its2 = [jnp.exp(others[k] - top) for k in range(2)]
        if it > 0:
            line = ext[it] + (ext_got[it, 0] + (ext_got[it, 1] + ext_got[it, 2]))
            anchor = to_column(line, B)

        @pl.loop(0, PAIRS)
        def _(t):
            if it == 0:
                for k in range(3):
                    row_copies(t, k).wait_recv()
            for k in range(2):
                p = 2 * t + k
                cols = slice(k * W, (k + 1) * W)
                m0, m1 = rows[t, 0:1, cols], rows_got[k, t, 0:1, cols]
                m = jnp.maximum(m0, m1)
                a, b = own1[k] * jnp.exp(m0 - m), its1[k] * jnp.exp(m1 - m)
                copy1(p, k).wait_recv()
                part2[it, p] = part1[it, p] * a + got1[it, p] * b
                copy2(p, k).start()

        tot[it] = jnp.zeros((GROUP, B + 8, 128), F32)
        if it == 0:
            small[2].wait()
        dims = (((1,), (1,)), ((), ()))

        def ratios(t, k, first_total):
            p = 2 * t + k
            cols = slice(k * W, (k + 1) * W)
            ms = [rows[t, 0:1, cols]] + [rows_got[j, t, 0:1, cols] for j in range(3)]
            pair = jnp.maximum(ms[0], ms[1 + k])
            other = jnp.maximum(ms[2 - k], ms[3])
            m = jnp.maximum(pair, other)
            a, b = own2[k] * jnp.exp(pair - m), its2[k] * jnp.exp(other - m)
            own_scale = jnp.exp(ms[0] - m)
            whole = pl.ds(pl.multiple_of(p * W, W), W)
            weight = counts[:, whole].astype(F32)
            if last:
                e0 = rows[t, 1:2, cols] + rows_got[0, t, 1:2, cols] + rows_got[1, t, 1:2, cols] + rows_got[2, t, 1:2, cols]
                first_boltz = jnp.exp(-e0 - m)
            copy2(p, k).wait_recv()
            denom = part2[it, p] * a + got2[it, p] * b
            ratio = weight / denom
            high, low = split(ratio * own_scale)
            rhs[k, 0:B, :] = high
            rhs[k, B : 2 * B, :] = low
            if last:
                lw_ref[:, whole] = denom
                first_terms = ratio * first_boltz
                first_total = first_total + (first_terms[:, :128] + first_terms[:, 128:])
            return first_total

        def terms(p, k, x):
            at = pl.ds(pl.multiple_of(x * 256, 256), 256)
            both = lax.dot_general(rhs[k], bh[p, at, :], dims, preferred_element_type=F32)
            rest = lax.dot_general(rhs[k, 0:B, :], bl[p, at, :], dims, preferred_element_type=F32)
            made = both[0:B] + (both[B : 2 * B] + rest)
            for core in range(2):
                j = 2 * x + core
                tot[it, j, 0:B, :] = tot[it, j, 0:B, :] + made[:, 128 * core : 128 * (core + 1)]

        def both_pieces(t, first_total):
            for k in range(2):
                first_total = ratios(t, k, first_total)
                for x in range(GROUP // 2):
                    terms(2 * t + k, k, x)
            return first_total

        first_total = lax.fori_loop(0, PAIRS - 1, both_pieces, jnp.zeros((B, 128), F32))
        first_total = ratios(PAIRS - 1, 0, first_total)
        for x in range(GROUP // 2):
            terms(PIECES - 2, 0, x)
        first_total = ratios(PAIRS - 1, 1, first_total)

        height = B + 1 if last else B
        span = pl.ds(0, height)
        if last:
            first_line = to_row(jnp.sum(first_total, axis=1, keepdims=True))
            for j in range(GROUP):
                tot[it, j, B : B + 1, :] = first_line
        scatter = []
        for ox in (2, 1, 3, 0):
            x = (g // 2 + ox) % (GROUP // 2)
            terms(PIECES - 1, 1, x)
            for oc in (0, 1):
                if ox == 0 and oc == 0:
                    continue
                slot = 2 * ox + oc
                to = 2 * x + (g + oc) % 2
                scatter.append((slot, send(tot.at[it, to, span], tot_got.at[it, slot, span], z * GROUP + to, y)))
        if it == 0:
            wait_rows()
        wait_parts()
        acc = tot[it, g, 0:height, :]
        for slot, copy in scatter[::-1]:
            copy.wait_recv()
            acc = acc + tot_got[it, slot, 0:height, :]
        ring[it, 0:height, :] = acc
        around = []
        for o in (4, 3, 5, 2, 6, 1, 7):
            around.append(send(ring.at[it, span], ring_got.at[it, z, span], ((z + o) % RING) * GROUP + g, y))
        ring_got[it, z, 0:height, :] = acc
        drain()
        if last:

            @pl.loop(0, PIECES)
            def _(p):
                whole = pl.ds(pl.multiple_of(p * W, W), W)
                lw_ref[:, whole] = jnp.log(lw_ref[:, whole]) + (top - anchor)

        for copy in around:
            copy.wait_recv()
        acc = ring_got[it, 0, 0:height, :]
        for k in range(1, RING):
            acc = acc + ring_got[it, k, 0:height, :]
        if last:
            value = jnp.log(to_column(acc[B : B + 1])) - jnp.log(acc[0:B])
        else:
            value = top - jnp.log(acc)
        val[it] = value
        gather = []
        for ox, oc in ((2, 0), (2, 1), (1, 0), (1, 1), (3, 0), (3, 1), (0, 1)):
            to = 2 * ((g // 2 + ox) % (GROUP // 2)) + (g + oc) % 2
            gather.append(send(val.at[it], val_got.at[it, g], z * GROUP + to, y))
        val_got[it, g] = value
        for copy in gather:
            copy.wait_recv()
        for j in range(GROUP):
            cols = pl.ds(128 * j, 128)
            if last:
                free_ref[:, cols] = val_got[it, j]
            else:
                lifted[:, cols] = val_got[it, j] + log_samples[j : j + 1, :]
    drain()


def finish(free_in, lw_in, free_out, lw_out):
    free_out[...] = free_in[...]
    lw_out[...] = lw_in[...]


def per_device(energies, samples, counts, initial):
    outside = pl.BlockSpec(memory_space=pl.ANY)
    inside = pl.BlockSpec(memory_space=pltpu.VMEM)
    copies = 3 * PAIRS + ITERS * (3 + 2 * PIECES + 2 * (GROUP - 1) + RING - 1)
    vmem = pltpu.VMEM
    free, log_weight = pl.pallas_call(
        kernel,
        out_shape=tuple(jax.ShapeDtypeStruct((B, n), F32) for n in (KS, NS)),
        in_specs=[outside] * 4,
        out_specs=(inside,) * 2,
        scratch_shapes=[
            vmem((PIECES, KS, W), F32),
            vmem((PIECES, KS, W), BF16),
            vmem((PIECES, KS, W), BF16),
            vmem((GROUP, 128), jnp.int32),
            vmem((B, NS), jnp.int32),
            vmem((B, KS), F32),
            vmem((2 * B, KS), BF16),
            vmem((2, 2 * B, W), BF16),
            vmem((B, 128), F32),
            vmem((GROUP, 128), F32),
            vmem((ITERS, PIECES, B, W), F32),
            vmem((ITERS, PIECES, B, W), F32),
            vmem((ITERS, PIECES, B, W), F32),
            vmem((ITERS, PIECES, B, W), F32),
            vmem((ITERS, 1, 128), F32),
            vmem((ITERS, 3, 1, 128), F32),
            vmem((PAIRS, 2, 2 * W), F32),
            vmem((3, PAIRS, 2, 2 * W), F32),
            vmem((ITERS, GROUP, B + 8, 128), F32),
            vmem((ITERS, GROUP, B + 8, 128), F32),
            vmem((ITERS, B + 8, 128), F32),
            vmem((ITERS, RING, B + 8, 128), F32),
            vmem((ITERS, B, 128), F32),
            vmem((ITERS, GROUP, B, 128), F32),
            pltpu.SemaphoreType.DMA((PIECES,)),
            pltpu.SemaphoreType.DMA((3,)),
            pltpu.SemaphoreType.DMA((copies,)),
            pltpu.SemaphoreType.DMA((copies,)),
        ],
        compiler_params=pltpu.CompilerParams(
            collective_id=0, has_side_effects=True, vmem_limit_bytes=56 * 2**20
        ),
    )(energies, samples.reshape(GROUP, 128), counts, initial)
    return pl.pallas_call(
        finish,
        out_shape=(jax.ShapeDtypeStruct((B, KS), F32), jax.ShapeDtypeStruct((B, NS), F32)),
        in_specs=[inside] * 2,
        out_specs=(inside,) * 2,
    )(free, log_weight)


def solution(mesh):
    in_specs = (P("state", "conf"), P("state"), P(None, "conf"), P(None, "state"))
    out_specs = (P(None, "state"), P(None, "conf"))
    return jax.shard_map(
        per_device, mesh=mesh, in_specs=in_specs, out_specs=out_specs, check_vma=False
    )
```

```python
import functools

import jax
import jax.numpy as jnp
from jax import lax
from jax.experimental import pallas as pl
from jax.experimental.pallas import tpu as pltpu
from jax.sharding import PartitionSpec as P

MESH = pl.DeviceIdType.MESH
ITERS = 2
B = 32
KS = 1024
NS = 2048
PIECES = 8
W = NS // PIECES
PAIRS = PIECES // 2
HELD = 1
DEEP = 256
GROUP = 8
RING = 8
F32 = jnp.float32
BF16 = jnp.bfloat16


def diagonal(offset):
    return lax.broadcasted_iota(jnp.int32, (B, 128), 1) == lax.broadcasted_iota(jnp.int32, (B, 128), 0) + offset


def to_row(column, offset=0):
    return jnp.sum(jnp.where(diagonal(offset), column, 0.0), axis=0, keepdims=True)


def to_column(row, offset=0):
    return jnp.sum(jnp.where(diagonal(offset), row, 0.0), axis=1, keepdims=True)


def split(x):
    high = x.astype(BF16)
    low = (x - high.astype(F32)).astype(BF16)
    return high, low


def kernel(
    e_hbm, samples_hbm, counts_hbm, initial_hbm, free_ref, lw_ref,
    e_buf, bh, bl, samples, counts, lifted, lhs, rhs, mine, log_samples,
    part1, part2, got1, got2, ext, ext_got, rows, rows_got, tot, tot_got, ring, ring_got, val, val_got,
    load_sem, small_sem, send_sem, recv_sem,
):
    c = lax.axis_index("conf")
    y = lax.axis_index("state")
    z, g = c // GROUP, c % GROUP
    peers = (y + 1 - 2 * (y % 2), 3 - y, (y + 2) % 4)

    small = [
        pltpu.make_async_copy(samples_hbm, samples, small_sem.at[0]),
        pltpu.make_async_copy(initial_hbm, lifted, small_sem.at[1]),
        pltpu.make_async_copy(counts_hbm, counts, small_sem.at[2]),
    ]
    small[0].start()
    small[1].start()
    loads = [pltpu.make_async_copy(e_hbm.at[:, pl.ds(p * W, W)], e_buf.at[p], load_sem.at[p]) for p in range(PIECES)]
    for copy in loads:
        copy.start()
    small[2].start()

    barrier = pltpu.get_barrier_semaphore()
    for peer in peers:
        pl.semaphore_signal(barrier, inc=1, device_id={"conf": c, "state": peer}, device_id_type=MESH)
    for o in range(1, GROUP):
        peer = z * GROUP + (g + o) % GROUP
        pl.semaphore_signal(barrier, inc=1, device_id={"conf": peer, "state": y}, device_id_type=MESH)
    for o in range(1, RING):
        peer = ((z + o) % RING) * GROUP + g
        pl.semaphore_signal(barrier, inc=1, device_id={"conf": peer, "state": y}, device_id_type=MESH)

    def remote(src, dst, conf, state, n):
        return pltpu.make_async_remote_copy(
            src_ref=src, dst_ref=dst, send_sem=send_sem.at[n], recv_sem=recv_sem.at[n],
            device_id={"conf": conf, "state": state}, device_id_type=MESH,
        )

    used = [0]

    def take(n):
        used[0] += n
        return used[0] - n

    undrained = []

    def send(src, dst, conf, state):
        copy = remote(src, dst, conf, state, take(1))
        copy.start()
        undrained.append(copy.wait_send)
        return copy

    def drain():
        for wait in undrained:
            wait()
        undrained.clear()

    def row_copies(t, k):
        return remote(rows.at[t], rows_got.at[k, t], c, peers[k], row_base + 3 * t + k)

    def wait_rows():
        @pl.loop(0, PAIRS)
        def _(t):
            for k in range(3):
                row_copies(t, k).wait_send()

    def send_rows(t):
        for k in (2, 0, 1):
            row_copies(t, k).start()

    row_base = take(3 * PAIRS)

    small[0].wait()
    small[1].wait()
    log_samples[...] = jnp.log(samples[...].astype(F32))
    for j in range(GROUP):
        cols = pl.ds(128 * j, 128)
        lifted[:, cols] = lifted[:, cols] + log_samples[j : j + 1, :]

    for it in range(ITERS):
        last = it == ITERS - 1
        top_me = jnp.max(lifted[...], axis=1, keepdims=True)
        mine[...] = jnp.broadcast_to(top_me, (B, 128))
        high, low = split(jnp.exp(lifted[...] - top_me))
        lhs[0:B, :] = high
        lhs[B : 2 * B, :] = low
        line = to_row(top_me)
        if it > 0:
            line = line + to_row(jnp.where(y == 0, val_got[it - 1, 0, :, 0:1], jnp.zeros((B, 1), F32)), B)
        ext[it] = line
        base1, base2 = take(PIECES), take(PIECES)

        def copy1(p, k):
            return remote(part1.at[it, p], got1.at[it, p], c, peers[k], base1 + p)

        def copy2(p, k):
            return remote(part2.at[it, p], got2.at[it, p], c, peers[1 - k], base2 + p)

        def wait_parts():
            @pl.loop(0, PAIRS)
            def _(t):
                for k in range(2):
                    copy1(2 * t + k, k).wait_send()
                    copy2(2 * t + k, k).wait_send()

        def products(t, sending):
            leasts = []
            if it == 0:
                for k in range(2):
                    p = 2 * t + k
                    pltpu.make_async_copy(e_hbm.at[:, pl.ds(0, W)], e_buf.at[p], load_sem.at[p]).wait()

                    def low_energy(r, acc):
                        return jnp.minimum(acc, jnp.min(e_buf[p, pl.ds(r * 64, 64), :].reshape(8, 8, W), axis=0))

                    least = lax.fori_loop(0, KS // 64, low_energy, jnp.full((8, W), jnp.inf, F32), unroll=16)
                    least = jnp.min(least, axis=0, keepdims=True)
                    cols = slice(k * W, (k + 1) * W)
                    rows[t, 0:1, cols] = -least
                    rows[t, 1:2, cols] = jnp.where(y == 0, e_buf[p, 0:1, :], jnp.zeros((1, W), F32))
                    leasts.append(least)
                if sending:
                    send_rows(t)
            for k in range(2):
                p = 2 * t + k
                if it == 0:
                    acc = jnp.zeros((B, W), F32)
                    for d in range(KS // DEEP):
                        for r in range(d * DEEP, (d + 1) * DEEP, 32):
                            high, low = split(jnp.exp(leasts[k] - e_buf[p, r : r + 32, :]))
                            bh[p, r : r + 32, :] = high
                            bl[p, r : r + 32, :] = low
                        at = slice(d * DEEP, (d + 1) * DEEP)
                        both = jnp.dot(lhs[:, at], bh[p, at, :], preferred_element_type=F32)
                        rest = jnp.dot(lhs[0:B, at], bl[p, at, :], preferred_element_type=F32)
                        acc = acc + (both[0:B] + (both[B : 2 * B] + rest))
                    part1[it, p] = acc
                else:
                    both = jnp.dot(lhs[...], bh[p], preferred_element_type=F32)
                    rest = jnp.dot(lhs[0:B, :], bl[p], preferred_element_type=F32)
                    part1[it, p] = both[0:B] + (both[B : 2 * B] + rest)

            if sending:
                for k in range(2):
                    copy1(2 * t + k, k).start()

        held = HELD if it == 0 else 0
        if held:

            @pl.loop(0, held)
            def _(t):
                products(t, False)

        if it == 0:
            pl.semaphore_wait(barrier, 3 + GROUP - 1 + RING - 1)
        ext_copies = [send(ext.at[it], ext_got.at[it, k], c, peers[k]) for k in (2, 0, 1)]
        if held:

            @pl.loop(0, held)
            def _(t):
                send_rows(t)
                for k in range(2):
                    copy1(2 * t + k, k).start()

        if held < PAIRS:

            @pl.loop(held, PAIRS)
            def _(t):
                products(t, True)

        for copy in ext_copies:
            copy.wait_recv()
        tops = [mine[:, 0:1]] + [to_column(ext_got[it, k]) for k in range(3)]
        pairs = [jnp.maximum(tops[0], tops[1]), jnp.maximum(tops[0], tops[2])]
        others = [jnp.maximum(tops[2], tops[3]), jnp.maximum(tops[1], tops[3])]
        top = jnp.maximum(pairs[0], others[0])
        own1 = [jnp.exp(tops[0] - pairs[k]) for k in range(2)]
        its1 = [jnp.exp(tops[1 + k] - pairs[k]) for k in range(2)]
        own2 = [jnp.exp(pairs[k] - top) for k in range(2)]
        its2 = [jnp.exp(others[k] - top) for k in range(2)]
        if it > 0:
            line = ext[it] + (ext_got[it, 0] + (ext_got[it, 1] + ext_got[it, 2]))
            anchor = to_column(line, B)

        @pl.loop(0, PAIRS)
        def _(t):
            if it == 0:
                for k in range(3):
                    row_copies(t, k).wait_recv()
            for k in range(2):
                p = 2 * t + k
                cols = slice(k * W, (k + 1) * W)
                m0, m1 = rows[t, 0:1, cols], rows_got[k, t, 0:1, cols]
                m = jnp.maximum(m0, m1)
                a, b = own1[k] * jnp.exp(m0 - m), its1[k] * jnp.exp(m1 - m)
                copy1(p, k).wait_recv()
                part2[it, p] = part1[it, p] * a + got1[it, p] * b
                copy2(p, k).start()

        tot[it] = jnp.zeros((GROUP, B + 8, 128), F32)
        if it == 0:
            small[2].wait()
        dims = (((1,), (1,)), ((), ()))

        def ratios(t, k, first_total):
            p = 2 * t + k
            cols = slice(k * W, (k + 1) * W)
            ms = [rows[t, 0:1, cols]] + [rows_got[j, t, 0:1, cols] for j in range(3)]
            pair = jnp.maximum(ms[0], ms[1 + k])
            other = jnp.maximum(ms[2 - k], ms[3])
            m = jnp.maximum(pair, other)
            a, b = own2[k] * jnp.exp(pair - m), its2[k] * jnp.exp(other - m)
            own_scale = jnp.exp(ms[0] - m)
            whole = pl.ds(pl.multiple_of(p * W, W), W)
            weight = counts[:, whole].astype(F32)
            if last:
                e0 = rows[t, 1:2, cols] + rows_got[0, t, 1:2, cols] + rows_got[1, t, 1:2, cols] + rows_got[2, t, 1:2, cols]
                first_boltz = jnp.exp(-e0 - m)
            if k == 0:
                copy2(p, 0).wait_recv()
                copy2(p + 1, 1).wait_recv()
            denom = part2[it, p] * a + got2[it, p] * b
            ratio = weight / denom
            high, low = split(ratio * own_scale)
            rhs[k, 0:B, :] = high
            rhs[k, B : 2 * B, :] = low
            if last:
                lw_ref[:, whole] = denom
                first_terms = ratio * first_boltz
                first_total = first_total + (first_terms[:, :128] + first_terms[:, 128:])
            return first_total

        def terms(t, x):
            at = pl.ds(pl.multiple_of(x * 256, 256), 256)
            both = [lax.dot_general(rhs[k], bh[2 * t + k, at, :], dims, preferred_element_type=F32) for k in range(2)]
            rest = [lax.dot_general(rhs[k, 0:B, :], bl[2 * t + k, at, :], dims, preferred_element_type=F32) for k in range(2)]
            made = both[0] + both[1]
            made = made[0:B] + (made[B : 2 * B] + (rest[0] + rest[1]))
            for core in range(2):
                j = 2 * x + core
                tot[it, j, 0:B, :] = tot[it, j, 0:B, :] + made[:, 128 * core : 128 * (core + 1)]

        def both_pieces(t, first_total):
            for k in range(2):
                first_total = ratios(t, k, first_total)
            for x in range(GROUP // 2):
                terms(t, x)
            return first_total

        first_total = lax.fori_loop(0, PAIRS - 1, both_pieces, jnp.zeros((B, 128), F32))
        for k in range(2):
            first_total = ratios(PAIRS - 1, k, first_total)

        height = B + 1 if last else B
        span = pl.ds(0, height)
        if last:
            first_line = to_row(jnp.sum(first_total, axis=1, keepdims=True))
            for j in range(GROUP):
                tot[it, j, B : B + 1, :] = first_line
        scatter = []
        for ox in (2, 1, 3, 0):
            x = (g // 2 + ox) % (GROUP // 2)
            terms(PAIRS - 1, x)
            for oc in (0, 1):
                if ox == 0 and oc == 0:
                    continue
                slot = 2 * ox + oc
                to = 2 * x + (g + oc) % 2
                scatter.append((slot, send(tot.at[it, to, span], tot_got.at[it, slot, span], z * GROUP + to, y)))
        acc = tot[it, g, 0:height, :]
        for slot, copy in scatter[::-1]:
            copy.wait_recv()
            acc = acc + tot_got[it, slot, 0:height, :]
        ring[it, 0:height, :] = acc
        around = []
        for o in (4, 3, 5, 2, 6, 1, 7):
            around.append(send(ring.at[it, span], ring_got.at[it, z, span], ((z + o) % RING) * GROUP + g, y))
        ring_got[it, z, 0:height, :] = acc
        if it == 0:
            wait_rows()
        wait_parts()
        drain()
        if last:

            @pl.loop(0, PIECES)
            def _(p):
                whole = pl.ds(pl.multiple_of(p * W, W), W)
                lw_ref[:, whole] = jnp.log(lw_ref[:, whole]) + (top - anchor)

        for copy in around:
            copy.wait_recv()
        acc = ring_got[it, 0, 0:height, :]
        for k in range(1, RING):
            acc = acc + ring_got[it, k, 0:height, :]
        if last:
            value = jnp.log(to_column(acc[B : B + 1])) - jnp.log(acc[0:B])
        else:
            value = top - jnp.log(acc)
        val[it] = value
        gather = []
        for ox, oc in ((2, 0), (2, 1), (1, 0), (1, 1), (3, 0), (3, 1), (0, 1)):
            to = 2 * ((g // 2 + ox) % (GROUP // 2)) + (g + oc) % 2
            gather.append(send(val.at[it], val_got.at[it, g], z * GROUP + to, y))
        val_got[it, g] = value
        for copy in gather:
            copy.wait_recv()
        for j in range(GROUP):
            cols = pl.ds(128 * j, 128)
            if last:
                free_ref[:, cols] = val_got[it, j]
            else:
                lifted[:, cols] = val_got[it, j] + log_samples[j : j + 1, :]
    drain()


def finish(free_in, lw_in, free_out, lw_out):
    free_out[...] = free_in[...]
    lw_out[...] = lw_in[...]


def per_device(energies, samples, counts, initial):
    outside = pl.BlockSpec(memory_space=pl.ANY)
    inside = pl.BlockSpec(memory_space=pltpu.VMEM)
    copies = 3 * PAIRS + ITERS * (3 + 2 * PIECES + 2 * (GROUP - 1) + RING - 1)
    vmem = pltpu.VMEM
    free, log_weight = pl.pallas_call(
        kernel,
        out_shape=tuple(jax.ShapeDtypeStruct((B, n), F32) for n in (KS, NS)),
        in_specs=[outside] * 4,
        out_specs=(inside,) * 2,
        scratch_shapes=[
            vmem((PIECES, KS, W), F32),
            vmem((PIECES, KS, W), BF16),
            vmem((PIECES, KS, W), BF16),
            vmem((GROUP, 128), jnp.int32),
            vmem((B, NS), jnp.int32),
            vmem((B, KS), F32),
            vmem((2 * B, KS), BF16),
            vmem((2, 2 * B, W), BF16),
            vmem((B, 128), F32),
            vmem((GROUP, 128), F32),
            vmem((ITERS, PIECES, B, W), F32),
            vmem((ITERS, PIECES, B, W), F32),
            vmem((ITERS, PIECES, B, W), F32),
            vmem((ITERS, PIECES, B, W), F32),
            vmem((ITERS, 1, 128), F32),
            vmem((ITERS, 3, 1, 128), F32),
            vmem((PAIRS, 2, 2 * W), F32),
            vmem((3, PAIRS, 2, 2 * W), F32),
            vmem((ITERS, GROUP, B + 8, 128), F32),
            vmem((ITERS, GROUP, B + 8, 128), F32),
            vmem((ITERS, B + 8, 128), F32),
            vmem((ITERS, RING, B + 8, 128), F32),
            vmem((ITERS, B, 128), F32),
            vmem((ITERS, GROUP, B, 128), F32),
            pltpu.SemaphoreType.DMA((PIECES,)),
            pltpu.SemaphoreType.DMA((3,)),
            pltpu.SemaphoreType.DMA((copies,)),
            pltpu.SemaphoreType.DMA((copies,)),
        ],
        compiler_params=pltpu.CompilerParams(
            collective_id=0, has_side_effects=True, vmem_limit_bytes=56 * 2**20
        ),
    )(energies, samples.reshape(GROUP, 128), counts, initial)
    return pl.pallas_call(
        finish,
        out_shape=(jax.ShapeDtypeStruct((B, KS), F32), jax.ShapeDtypeStruct((B, NS), F32)),
        in_specs=[inside] * 2,
        out_specs=(inside,) * 2,
    )(free, log_weight)


def solution(mesh):
    in_specs = (P("state", "conf"), P("state"), P(None, "conf"), P(None, "state"))
    out_specs = (P(None, "state"), P(None, "conf"))
    return jax.shard_map(
        per_device, mesh=mesh, in_specs=in_specs, out_specs=out_specs, check_vma=False
    )
```

```python
import functools

import jax
import jax.numpy as jnp
from jax import lax
from jax.experimental import pallas as pl
from jax.experimental.pallas import tpu as pltpu
from jax.sharding import PartitionSpec as P

MESH = pl.DeviceIdType.MESH
ITERS = 2
B = 32
KS = 1024
NS = 2048
PIECES = 8
W = NS // PIECES
PAIRS = PIECES // 2
HELD = 1
DEEP = 256
GROUP = 8
RING = 8
F32 = jnp.float32
BF16 = jnp.bfloat16


def diagonal(offset):
    return lax.broadcasted_iota(jnp.int32, (B, 128), 1) == lax.broadcasted_iota(jnp.int32, (B, 128), 0) + offset


def to_row(column, offset=0):
    return jnp.sum(jnp.where(diagonal(offset), column, 0.0), axis=0, keepdims=True)


def to_column(row, offset=0):
    return jnp.sum(jnp.where(diagonal(offset), row, 0.0), axis=1, keepdims=True)


def split(x):
    high = x.astype(BF16)
    low = (x - high.astype(F32)).astype(BF16)
    return high, low


def kernel(
    e_hbm, samples_hbm, counts_hbm, initial_hbm, free_ref, lw_ref,
    e_buf, bh, bl, samples, counts, lifted, lhs, rhs, mine, log_samples,
    part1, part2, got1, got2, ext, ext_got, rows, rows_got, tot, tot_got, ring, ring_got, val, val_got,
    load_sem, small_sem, send_sem, recv_sem,
):
    c = lax.axis_index("conf")
    y = lax.axis_index("state")
    z, g = c // GROUP, c % GROUP
    peers = (y + 1 - 2 * (y % 2), 3 - y, (y + 2) % 4)

    small = [
        pltpu.make_async_copy(samples_hbm, samples, small_sem.at[0]),
        pltpu.make_async_copy(initial_hbm, lifted, small_sem.at[1]),
        pltpu.make_async_copy(counts_hbm, counts, small_sem.at[2]),
    ]
    small[0].start()
    small[1].start()
    loads = [pltpu.make_async_copy(e_hbm.at[:, pl.ds(p * W, W)], e_buf.at[p], load_sem.at[p]) for p in range(PIECES)]
    for copy in loads:
        copy.start()
    small[2].start()

    barrier = pltpu.get_barrier_semaphore()
    for o in (4, 3, 5, 2, 6, 1, 7):
        peer = ((z + o) % RING) * GROUP + g
        pl.semaphore_signal(barrier, inc=1, device_id={"conf": peer, "state": y}, device_id_type=MESH)
    for o in (4, 5, 2, 3, 6, 7, 1):
        peer = z * GROUP + (g + o) % GROUP
        pl.semaphore_signal(barrier, inc=1, device_id={"conf": peer, "state": y}, device_id_type=MESH)
    for peer in peers[::-1]:
        pl.semaphore_signal(barrier, inc=1, device_id={"conf": c, "state": peer}, device_id_type=MESH)

    def remote(src, dst, conf, state, n):
        return pltpu.make_async_remote_copy(
            src_ref=src, dst_ref=dst, send_sem=send_sem.at[n], recv_sem=recv_sem.at[n],
            device_id={"conf": conf, "state": state}, device_id_type=MESH,
        )

    used = [0]

    def take(n):
        used[0] += n
        return used[0] - n

    undrained = []

    def send(src, dst, conf, state):
        copy = remote(src, dst, conf, state, take(1))
        copy.start()
        undrained.append(copy.wait_send)
        return copy

    def drain():
        for wait in undrained:
            wait()
        undrained.clear()

    def row_copies(t, k):
        return remote(rows.at[t], rows_got.at[k, t], c, peers[k], row_base + 3 * t + k)

    def wait_rows():
        @pl.loop(0, PAIRS)
        def _(t):
            for k in range(3):
                row_copies(t, k).wait_send()

    def send_rows(t):
        for k in (2, 0, 1):
            row_copies(t, k).start()

    row_base = take(3 * PAIRS)

    small[0].wait()
    small[1].wait()
    log_samples[...] = jnp.log(samples[...].astype(F32))
    for j in range(GROUP):
        cols = pl.ds(128 * j, 128)
        lifted[:, cols] = lifted[:, cols] + log_samples[j : j + 1, :]

    for it in range(ITERS):
        last = it == ITERS - 1
        top_me = jnp.max(lifted[...], axis=1, keepdims=True)
        mine[...] = jnp.broadcast_to(top_me, (B, 128))
        high, low = split(jnp.exp(lifted[...] - top_me))
        lhs[0:B, :] = high
        lhs[B : 2 * B, :] = low
        line = to_row(top_me)
        if it > 0:
            line = line + to_row(jnp.where(y == 0, val_got[it - 1, 0, :, 0:1], jnp.zeros((B, 1), F32)), B)
        ext[it] = line
        base1, base2 = take(PIECES), take(PIECES)

        def copy1(p, k):
            return remote(part1.at[it, p], got1.at[it, p], c, peers[k], base1 + p)

        def copy2(p, k):
            return remote(part2.at[it, p], got2.at[it, p], c, peers[1 - k], base2 + p)

        def wait_parts():
            @pl.loop(0, PAIRS)
            def _(t):
                for k in range(2):
                    copy1(2 * t + k, k).wait_send()
                    copy2(2 * t + k, k).wait_send()

        def products(t, sending):
            leasts = []
            if it == 0:
                for k in range(2):
                    p = 2 * t + k
                    pltpu.make_async_copy(e_hbm.at[:, pl.ds(0, W)], e_buf.at[p], load_sem.at[p]).wait()

                    def low_energy(r, acc):
                        return jnp.minimum(acc, jnp.min(e_buf[p, pl.ds(r * 64, 64), :].reshape(8, 8, W), axis=0))

                    least = lax.fori_loop(0, KS // 64, low_energy, jnp.full((8, W), jnp.inf, F32), unroll=16)
                    least = jnp.min(least, axis=0, keepdims=True)
                    cols = slice(k * W, (k + 1) * W)
                    rows[t, 0:1, cols] = -least
                    rows[t, 1:2, cols] = jnp.where(y == 0, e_buf[p, 0:1, :], jnp.zeros((1, W), F32))
                    leasts.append(least)
                if sending:
                    send_rows(t)
            for k in range(2):
                p = 2 * t + k
                if it == 0:
                    acc = jnp.zeros((B, W), F32)
                    for d in range(KS // DEEP):
                        for r in range(d * DEEP, (d + 1) * DEEP, 32):
                            high, low = split(jnp.exp(leasts[k] - e_buf[p, r : r + 32, :]))
                            bh[p, r : r + 32, :] = high
                            bl[p, r : r + 32, :] = low
                        at = slice(d * DEEP, (d + 1) * DEEP)
                        both = jnp.dot(lhs[:, at], bh[p, at, :], preferred_element_type=F32)
                        rest = jnp.dot(lhs[0:B, at], bl[p, at, :], preferred_element_type=F32)
                        acc = acc + (both[0:B] + (both[B : 2 * B] + rest))
                    part1[it, p] = acc
                else:
                    both = jnp.dot(lhs[...], bh[p], preferred_element_type=F32)
                    rest = jnp.dot(lhs[0:B, :], bl[p], preferred_element_type=F32)
                    part1[it, p] = both[0:B] + (both[B : 2 * B] + rest)

            if sending:
                for k in range(2):
                    copy1(2 * t + k, k).start()

        held = HELD if it == 0 else 0
        if held:

            @pl.loop(0, held)
            def _(t):
                products(t, False)

        if it == 0:
            pl.semaphore_wait(barrier, 3 + GROUP - 1 + RING - 1)
        ext_copies = [send(ext.at[it], ext_got.at[it, k], c, peers[k]) for k in (2, 0, 1)]
        if held:

            @pl.loop(0, held)
            def _(t):
                send_rows(t)
                for k in range(2):
                    copy1(2 * t + k, k).start()

        if held < PAIRS:

            @pl.loop(held, PAIRS)
            def _(t):
                products(t, True)

        for copy in ext_copies:
            copy.wait_recv()
        tops = [mine[:, 0:1]] + [to_column(ext_got[it, k]) for k in range(3)]
        pairs = [jnp.maximum(tops[0], tops[1]), jnp.maximum(tops[0], tops[2])]
        others = [jnp.maximum(tops[2], tops[3]), jnp.maximum(tops[1], tops[3])]
        top = jnp.maximum(pairs[0], others[0])
        own1 = [jnp.exp(tops[0] - pairs[k]) for k in range(2)]
        its1 = [jnp.exp(tops[1 + k] - pairs[k]) for k in range(2)]
        own2 = [jnp.exp(pairs[k] - top) for k in range(2)]
        its2 = [jnp.exp(others[k] - top) for k in range(2)]
        if it > 0:
            line = ext[it] + (ext_got[it, 0] + (ext_got[it, 1] + ext_got[it, 2]))
            anchor = to_column(line, B)

        @pl.loop(0, PAIRS)
        def _(t):
            if it == 0:
                for k in range(3):
                    row_copies(t, k).wait_recv()
            for k in range(2):
                p = 2 * t + k
                cols = slice(k * W, (k + 1) * W)
                m0, m1 = rows[t, 0:1, cols], rows_got[k, t, 0:1, cols]
                m = jnp.maximum(m0, m1)
                a, b = own1[k] * jnp.exp(m0 - m), its1[k] * jnp.exp(m1 - m)
                copy1(p, k).wait_recv()
                part2[it, p] = part1[it, p] * a + got1[it, p] * b
                copy2(p, k).start()

        tot[it] = jnp.zeros((GROUP, B + 8, 128), F32)
        if it == 0:
            small[2].wait()
        dims = (((1,), (1,)), ((), ()))

        def ratios(t, k, first_total):
            p = 2 * t + k
            cols = slice(k * W, (k + 1) * W)
            ms = [rows[t, 0:1, cols]] + [rows_got[j, t, 0:1, cols] for j in range(3)]
            pair = jnp.maximum(ms[0], ms[1 + k])
            other = jnp.maximum(ms[2 - k], ms[3])
            m = jnp.maximum(pair, other)
            a, b = own2[k] * jnp.exp(pair - m), its2[k] * jnp.exp(other - m)
            own_scale = jnp.exp(ms[0] - m)
            whole = pl.ds(pl.multiple_of(p * W, W), W)
            weight = counts[:, whole].astype(F32)
            if last:
                e0 = rows[t, 1:2, cols] + rows_got[0, t, 1:2, cols] + rows_got[1, t, 1:2, cols] + rows_got[2, t, 1:2, cols]
                first_boltz = jnp.exp(-e0 - m)
            if k == 0:
                copy2(p, 0).wait_recv()
                copy2(p + 1, 1).wait_recv()
            denom = part2[it, p] * a + got2[it, p] * b
            ratio = weight / denom
            high, low = split(ratio * own_scale)
            rhs[k, 0:B, :] = high
            rhs[k, B : 2 * B, :] = low
            if last:
                lw_ref[:, whole] = denom
                first_terms = ratio * first_boltz
                first_total = first_total + (first_terms[:, :128] + first_terms[:, 128:])
            return first_total

        def terms(t, x):
            at = pl.ds(pl.multiple_of(x * 256, 256), 256)
            both = [lax.dot_general(rhs[k], bh[2 * t + k, at, :], dims, preferred_element_type=F32) for k in range(2)]
            rest = [lax.dot_general(rhs[k, 0:B, :], bl[2 * t + k, at, :], dims, preferred_element_type=F32) for k in range(2)]
            made = both[0] + both[1]
            made = made[0:B] + (made[B : 2 * B] + (rest[0] + rest[1]))
            for core in range(2):
                j = 2 * x + core
                tot[it, j, 0:B, :] = tot[it, j, 0:B, :] + made[:, 128 * core : 128 * (core + 1)]

        def both_pieces(t, first_total):
            for k in range(2):
                first_total = ratios(t, k, first_total)
            for x in range(GROUP // 2):
                terms(t, x)
            return first_total

        first_total = lax.fori_loop(0, PAIRS - 1, both_pieces, jnp.zeros((B, 128), F32))
        for k in range(2):
            first_total = ratios(PAIRS - 1, k, first_total)

        height = B + 1 if last else B
        span = pl.ds(0, height)
        if last:
            first_line = to_row(jnp.sum(first_total, axis=1, keepdims=True))
            for j in range(GROUP):
                tot[it, j, B : B + 1, :] = first_line
        scatter = []
        for ox in (2, 1, 3, 0):
            x = (g // 2 + ox) % (GROUP // 2)
            terms(PAIRS - 1, x)
            for oc in (0, 1):
                if ox == 0 and oc == 0:
                    continue
                slot = 2 * ox + oc
                to = 2 * x + (g + oc) % 2
                scatter.append((slot, send(tot.at[it, to, span], tot_got.at[it, slot, span], z * GROUP + to, y)))
        if it == 0:
            wait_rows()
        wait_parts()
        acc = tot[it, g, 0:height, :]
        for slot, copy in scatter[::-1]:
            copy.wait_recv()
            acc = acc + tot_got[it, slot, 0:height, :]
        ring[it, 0:height, :] = acc
        around = []
        for o in (4, 3, 5, 2, 6, 1, 7):
            around.append(send(ring.at[it, span], ring_got.at[it, z, span], ((z + o) % RING) * GROUP + g, y))
        ring_got[it, z, 0:height, :] = acc
        drain()
        if last:

            @pl.loop(0, PIECES)
            def _(p):
                whole = pl.ds(pl.multiple_of(p * W, W), W)
                lw_ref[:, whole] = jnp.log(lw_ref[:, whole]) + (top - anchor)

        for copy in around:
            copy.wait_recv()
        acc = ring_got[it, 0, 0:height, :]
        for k in range(1, RING):
            acc = acc + ring_got[it, k, 0:height, :]
        if last:
            value = jnp.log(to_column(acc[B : B + 1])) - jnp.log(acc[0:B])
        else:
            value = top - jnp.log(acc)
        val[it] = value
        gather = []
        for ox, oc in ((2, 0), (2, 1), (1, 0), (1, 1), (3, 0), (3, 1), (0, 1)):
            to = 2 * ((g // 2 + ox) % (GROUP // 2)) + (g + oc) % 2
            gather.append(send(val.at[it], val_got.at[it, g], z * GROUP + to, y))
        val_got[it, g] = value
        for copy in gather:
            copy.wait_recv()
        for j in range(GROUP):
            cols = pl.ds(128 * j, 128)
            if last:
                free_ref[:, cols] = val_got[it, j]
            else:
                lifted[:, cols] = val_got[it, j] + log_samples[j : j + 1, :]
    drain()


def finish(free_in, lw_in, free_out, lw_out):
    free_out[...] = free_in[...]
    lw_out[...] = lw_in[...]


def per_device(energies, samples, counts, initial):
    outside = pl.BlockSpec(memory_space=pl.ANY)
    inside = pl.BlockSpec(memory_space=pltpu.VMEM)
    copies = 3 * PAIRS + ITERS * (3 + 2 * PIECES + 2 * (GROUP - 1) + RING - 1)
    vmem = pltpu.VMEM
    free, log_weight = pl.pallas_call(
        kernel,
        out_shape=tuple(jax.ShapeDtypeStruct((B, n), F32) for n in (KS, NS)),
        in_specs=[outside] * 4,
        out_specs=(inside,) * 2,
        scratch_shapes=[
            vmem((PIECES, KS, W), F32),
            vmem((PIECES, KS, W), BF16),
            vmem((PIECES, KS, W), BF16),
            vmem((GROUP, 128), jnp.int32),
            vmem((B, NS), jnp.int32),
            vmem((B, KS), F32),
            vmem((2 * B, KS), BF16),
            vmem((2, 2 * B, W), BF16),
            vmem((B, 128), F32),
            vmem((GROUP, 128), F32),
            vmem((ITERS, PIECES, B, W), F32),
            vmem((ITERS, PIECES, B, W), F32),
            vmem((ITERS, PIECES, B, W), F32),
            vmem((ITERS, PIECES, B, W), F32),
            vmem((ITERS, 1, 128), F32),
            vmem((ITERS, 3, 1, 128), F32),
            vmem((PAIRS, 2, 2 * W), F32),
            vmem((3, PAIRS, 2, 2 * W), F32),
            vmem((ITERS, GROUP, B + 8, 128), F32),
            vmem((ITERS, GROUP, B + 8, 128), F32),
            vmem((ITERS, B + 8, 128), F32),
            vmem((ITERS, RING, B + 8, 128), F32),
            vmem((ITERS, B, 128), F32),
            vmem((ITERS, GROUP, B, 128), F32),
            pltpu.SemaphoreType.DMA((PIECES,)),
            pltpu.SemaphoreType.DMA((3,)),
            pltpu.SemaphoreType.DMA((copies,)),
            pltpu.SemaphoreType.DMA((copies,)),
        ],
        compiler_params=pltpu.CompilerParams(
            collective_id=0, has_side_effects=True, vmem_limit_bytes=56 * 2**20
        ),
    )(energies, samples.reshape(GROUP, 128), counts, initial)
    return pl.pallas_call(
        finish,
        out_shape=(jax.ShapeDtypeStruct((B, KS), F32), jax.ShapeDtypeStruct((B, NS), F32)),
        in_specs=[inside] * 2,
        out_specs=(inside,) * 2,
    )(free, log_weight)


def solution(mesh):
    in_specs = (P("state", "conf"), P("state"), P(None, "conf"), P(None, "state"))
    out_specs = (P(None, "state"), P(None, "conf"))
    return jax.shard_map(
        per_device, mesh=mesh, in_specs=in_specs, out_specs=out_specs, check_vma=False
    )
```

```python
import functools

import jax
import jax.numpy as jnp
from jax import lax
from jax.experimental import pallas as pl
from jax.experimental.pallas import tpu as pltpu
from jax.sharding import PartitionSpec as P

MESH = pl.DeviceIdType.MESH
ITERS = 2
B = 32
KS = 1024
NS = 2048
PIECES = 8
W = NS // PIECES
PAIRS = PIECES // 2
HELD = 1
DEEP = 256
GROUP = 8
RING = 8
F32 = jnp.float32
BF16 = jnp.bfloat16


def diagonal(offset):
    return lax.broadcasted_iota(jnp.int32, (B, 128), 1) == lax.broadcasted_iota(jnp.int32, (B, 128), 0) + offset


def to_row(column, offset=0):
    return jnp.sum(jnp.where(diagonal(offset), column, 0.0), axis=0, keepdims=True)


def to_column(row, offset=0):
    return jnp.sum(jnp.where(diagonal(offset), row, 0.0), axis=1, keepdims=True)


def split(x):
    high = x.astype(BF16)
    low = (x - high.astype(F32)).astype(BF16)
    return high, low


def kernel(
    e_hbm, samples_hbm, counts_hbm, initial_hbm, free_ref, lw_ref,
    e_buf, bh, bl, samples, counts, lifted, lhs, rhs, mine, log_samples,
    part1, part2, got1, got2, ext, ext_got, rows, rows_got, tot, tot_got, ring, ring_got, val, val_got,
    load_sem, small_sem, send_sem, recv_sem,
):
    c = lax.axis_index("conf")
    y = lax.axis_index("state")
    z, g = c // GROUP, c % GROUP
    peers = (y + 1 - 2 * (y % 2), 3 - y, (y + 2) % 4)

    small = [
        pltpu.make_async_copy(samples_hbm, samples, small_sem.at[0]),
        pltpu.make_async_copy(initial_hbm, lifted, small_sem.at[1]),
        pltpu.make_async_copy(counts_hbm, counts, small_sem.at[2]),
    ]
    small[0].start()
    small[1].start()
    loads = [pltpu.make_async_copy(e_hbm.at[:, pl.ds(p * W, W)], e_buf.at[p], load_sem.at[p]) for p in range(PIECES)]
    for copy in loads:
        copy.start()
    small[2].start()

    barrier = pltpu.get_barrier_semaphore()
    for o in (4, 3, 5, 2, 6, 1, 7):
        peer = ((z + o) % RING) * GROUP + g
        pl.semaphore_signal(barrier, inc=1, device_id={"conf": peer, "state": y}, device_id_type=MESH)
    for o in (4, 5, 2, 3, 6, 7, 1):
        peer = z * GROUP + (g + o) % GROUP
        pl.semaphore_signal(barrier, inc=1, device_id={"conf": peer, "state": y}, device_id_type=MESH)
    for peer in peers[::-1]:
        pl.semaphore_signal(barrier, inc=1, device_id={"conf": c, "state": peer}, device_id_type=MESH)

    def remote(src, dst, conf, state, n):
        return pltpu.make_async_remote_copy(
            src_ref=src, dst_ref=dst, send_sem=send_sem.at[n], recv_sem=recv_sem.at[n],
            device_id={"conf": conf, "state": state}, device_id_type=MESH,
        )

    used = [0]

    def take(n):
        used[0] += n
        return used[0] - n

    undrained = []

    def send(src, dst, conf, state):
        copy = remote(src, dst, conf, state, take(1))
        copy.start()
        undrained.append(copy.wait_send)
        return copy

    def drain():
        for wait in undrained:
            wait()
        undrained.clear()

    def row_copies(t, k):
        return remote(rows.at[t], rows_got.at[k, t], c, peers[k], row_base + 3 * t + k)

    def wait_rows():
        @pl.loop(0, PAIRS)
        def _(t):
            for k in range(3):
                row_copies(t, k).wait_send()

    def send_rows(t):
        for k in (2, 0, 1):
            row_copies(t, k).start()

    row_base = take(3 * PAIRS)

    small[0].wait()
    small[1].wait()
    log_samples[...] = jnp.log(samples[...].astype(F32))
    for j in range(GROUP):
        cols = pl.ds(128 * j, 128)
        lifted[:, cols] = lifted[:, cols] + log_samples[j : j + 1, :]

    for it in range(ITERS):
        last = it == ITERS - 1
        top_me = jnp.max(lifted[...], axis=1, keepdims=True)
        mine[...] = jnp.broadcast_to(top_me, (B, 128))
        high, low = split(jnp.exp(lifted[...] - top_me))
        lhs[0:B, :] = high
        lhs[B : 2 * B, :] = low
        line = to_row(top_me)
        if it > 0:
            line = line + to_row(jnp.where(y == 0, val_got[it - 1, 0, :, 0:1], jnp.zeros((B, 1), F32)), B)
        ext[it] = line
        base1, base2 = take(PIECES), take(PIECES)

        def copy1(p, k):
            return remote(part1.at[it, p], got1.at[it, p], c, peers[k], base1 + p)

        def copy2(p, k):
            return remote(part2.at[it, p], got2.at[it, p], c, peers[1 - k], base2 + p)

        def wait_parts():
            @pl.loop(0, PAIRS)
            def _(t):
                for k in range(2):
                    copy1(2 * t + k, k).wait_send()
                    copy2(2 * t + k, k).wait_send()

        def products(t, sending):
            leasts = []
            if it == 0:
                for k in range(2):
                    p = 2 * t + k
                    pltpu.make_async_copy(e_hbm.at[:, pl.ds(0, W)], e_buf.at[p], load_sem.at[p]).wait()

                    def low_energy(r, acc):
                        return jnp.minimum(acc, jnp.min(e_buf[p, pl.ds(r * 64, 64), :].reshape(8, 8, W), axis=0))

                    least = lax.fori_loop(0, KS // 64, low_energy, jnp.full((8, W), jnp.inf, F32), unroll=16)
                    least = jnp.min(least, axis=0, keepdims=True)
                    cols = slice(k * W, (k + 1) * W)
                    rows[t, 0:1, cols] = -least
                    rows[t, 1:2, cols] = jnp.where(y == 0, e_buf[p, 0:1, :], jnp.zeros((1, W), F32))
                    leasts.append(least)
                if sending:
                    send_rows(t)
            for k in range(2):
                p = 2 * t + k
                if it == 0:
                    acc = jnp.zeros((B, W), F32)
                    for d in range(KS // DEEP):
                        for r in range(d * DEEP, (d + 1) * DEEP, 32):
                            high, low = split(jnp.exp(leasts[k] - e_buf[p, r : r + 32, :]))
                            bh[p, r : r + 32, :] = high
                            bl[p, r : r + 32, :] = low
                        at = slice(d * DEEP, (d + 1) * DEEP)
                        both = jnp.dot(lhs[:, at], bh[p, at, :], preferred_element_type=F32)
                        rest = jnp.dot(lhs[0:B, at], bl[p, at, :], preferred_element_type=F32)
                        acc = acc + (both[0:B] + (both[B : 2 * B] + rest))
                    part1[it, p] = acc
                else:
                    both = jnp.dot(lhs[...], bh[p], preferred_element_type=F32)
                    rest = jnp.dot(lhs[0:B, :], bl[p], preferred_element_type=F32)
                    part1[it, p] = both[0:B] + (both[B : 2 * B] + rest)

            if sending:
                for k in range(2):
                    copy1(2 * t + k, k).start()

        held = HELD if it == 0 else 0
        if held:

            @pl.loop(0, held)
            def _(t):
                products(t, False)

        if it == 0:
            pl.semaphore_wait(barrier, 3 + GROUP - 1 + RING - 1)
        ext_copies = [send(ext.at[it], ext_got.at[it, k], c, peers[k]) for k in (2, 0, 1)]
        if held:

            @pl.loop(0, held)
            def _(t):
                send_rows(t)
                for k in range(2):
                    copy1(2 * t + k, k).start()

        if held < PAIRS:

            @pl.loop(held, PAIRS)
            def _(t):
                products(t, True)

        for copy in ext_copies:
            copy.wait_recv()
        tops = [mine[:, 0:1]] + [to_column(ext_got[it, k]) for k in range(3)]
        pairs = [jnp.maximum(tops[0], tops[1]), jnp.maximum(tops[0], tops[2])]
        others = [jnp.maximum(tops[2], tops[3]), jnp.maximum(tops[1], tops[3])]
        top = jnp.maximum(pairs[0], others[0])
        own1 = [jnp.exp(tops[0] - pairs[k]) for k in range(2)]
        its1 = [jnp.exp(tops[1 + k] - pairs[k]) for k in range(2)]
        own2 = [jnp.exp(pairs[k] - top) for k in range(2)]
        its2 = [jnp.exp(others[k] - top) for k in range(2)]
        if it > 0:
            line = ext[it] + (ext_got[it, 0] + (ext_got[it, 1] + ext_got[it, 2]))
            anchor = to_column(line, B)

        @pl.loop(0, PAIRS)
        def _(t):
            if it == 0:
                for k in range(3):
                    row_copies(t, k).wait_recv()
            for k in range(2):
                p = 2 * t + k
                cols = slice(k * W, (k + 1) * W)
                m0, m1 = rows[t, 0:1, cols], rows_got[k, t, 0:1, cols]
                m = jnp.maximum(m0, m1)
                a, b = own1[k] * jnp.exp(m0 - m), its1[k] * jnp.exp(m1 - m)
                copy1(p, k).wait_recv()
                part2[it, p] = part1[it, p] * a + got1[it, p] * b
                copy2(p, k).start()

        tot[it] = jnp.zeros((GROUP, B + 8, 128), F32)
        if it == 0:
            small[2].wait()
        dims = (((1,), (1,)), ((), ()))

        def ratios(t, k, first_total):
            p = 2 * t + k
            cols = slice(k * W, (k + 1) * W)
            ms = [rows[t, 0:1, cols]] + [rows_got[j, t, 0:1, cols] for j in range(3)]
            pair = jnp.maximum(ms[0], ms[1 + k])
            other = jnp.maximum(ms[2 - k], ms[3])
            m = jnp.maximum(pair, other)
            a, b = own2[k] * jnp.exp(pair - m), its2[k] * jnp.exp(other - m)
            own_scale = jnp.exp(ms[0] - m)
            whole = pl.ds(pl.multiple_of(p * W, W), W)
            weight = counts[:, whole].astype(F32)
            if last:
                e0 = rows[t, 1:2, cols] + rows_got[0, t, 1:2, cols] + rows_got[1, t, 1:2, cols] + rows_got[2, t, 1:2, cols]
                first_boltz = jnp.exp(-e0 - m)
            if k == 0:
                copy2(p, 0).wait_recv()
                copy2(p + 1, 1).wait_recv()
            denom = part2[it, p] * a + got2[it, p] * b
            ratio = weight / denom
            high, low = split(ratio * own_scale)
            rhs[k, 0:B, :] = high
            rhs[k, B : 2 * B, :] = low
            if last:
                lw_ref[:, whole] = denom
                first_terms = ratio * first_boltz
                first_total = first_total + (first_terms[:, :128] + first_terms[:, 128:])
            return first_total

        def terms(t, x):
            at = pl.ds(pl.multiple_of(x * 256, 256), 256)
            both = [lax.dot_general(rhs[k], bh[2 * t + k, at, :], dims, preferred_element_type=F32) for k in range(2)]
            rest = [lax.dot_general(rhs[k, 0:B, :], bl[2 * t + k, at, :], dims, preferred_element_type=F32) for k in range(2)]
            made = both[0] + both[1]
            made = made[0:B] + (made[B : 2 * B] + (rest[0] + rest[1]))
            for core in range(2):
                j = 2 * x + core
                tot[it, j, 0:B, :] = tot[it, j, 0:B, :] + made[:, 128 * core : 128 * (core + 1)]

        def both_pieces(t, first_total):
            for k in range(2):
                first_total = ratios(t, k, first_total)
            for x in range(GROUP // 2):
                terms(t, x)
            return first_total

        first_total = lax.fori_loop(0, PAIRS - 1, both_pieces, jnp.zeros((B, 128), F32))
        for k in range(2):
            first_total = ratios(PAIRS - 1, k, first_total)

        height = B + 1 if last else B
        span = pl.ds(0, height)
        if last:
            first_line = to_row(jnp.sum(first_total, axis=1, keepdims=True))
            for j in range(GROUP):
                tot[it, j, B : B + 1, :] = first_line
        scatter = []
        for ox in (2, 1, 3, 0):
            x = (g // 2 + ox) % (GROUP // 2)
            terms(PAIRS - 1, x)
            for oc in (0, 1):
                if ox == 0 and oc == 0:
                    continue
                slot = 2 * ox + oc
                to = 2 * x + (g + oc) % 2
                scatter.append((slot, send(tot.at[it, to, span], tot_got.at[it, slot, span], z * GROUP + to, y)))
        if it == 0:
            wait_rows()
        wait_parts()
        acc = tot[it, g, 0:height, :]
        for slot, copy in scatter[::-1]:
            copy.wait_recv()
            acc = acc + tot_got[it, slot, 0:height, :]
        ring[it, 0:height, :] = acc
        around = []
        for o in (4, 3, 5, 2, 6, 1, 7):
            around.append(send(ring.at[it, span], ring_got.at[it, z, span], ((z + o) % RING) * GROUP + g, y))
        ring_got[it, z, 0:height, :] = acc
        drain()
        if last:

            @pl.loop(0, PIECES)
            def _(p):
                whole = pl.ds(pl.multiple_of(p * W, W), W)
                lw_ref[:, whole] = jnp.log(lw_ref[:, whole]) + (top - anchor)

        for copy in around:
            copy.wait_recv()
        acc = ring_got[it, 0, 0:height, :]
        for k in range(1, RING):
            acc = acc + ring_got[it, k, 0:height, :]
        if last:
            value = jnp.log(to_column(acc[B : B + 1])) - jnp.log(acc[0:B])
        else:
            value = top - jnp.log(acc)
        val[it] = value
        gather = []
        for ox, oc in ((2, 0), (2, 1), (1, 0), (1, 1), (3, 0), (3, 1), (0, 1)):
            to = 2 * ((g // 2 + ox) % (GROUP // 2)) + (g + oc) % 2
            gather.append(send(val.at[it], val_got.at[it, g], z * GROUP + to, y))
        val_got[it, g] = value
        for copy in gather:
            copy.wait_recv()
        for j in range(GROUP):
            cols = pl.ds(128 * j, 128)
            if last:
                free_ref[:, cols] = val_got[it, j]
            else:
                lifted[:, cols] = val_got[it, j] + log_samples[j : j + 1, :]
    drain()


def finish(free_in, lw_in, free_out, lw_out, free_buf, lw_buf, sem):
    steps = []
    for n, (src, buf, dst) in enumerate(((lw_in, lw_buf, lw_out), (free_in, free_buf, free_out))):
        steps.append((pltpu.make_async_copy(src, buf, sem.at[2 * n]), pltpu.make_async_copy(buf, dst, sem.at[2 * n + 1])))
    for come, _ in steps:
        come.start()
    for come, go in steps:
        come.wait()
        go.start()
    for _, go in steps:
        go.wait()


def per_device(energies, samples, counts, initial):
    outside = pl.BlockSpec(memory_space=pl.ANY)
    inside = pl.BlockSpec(memory_space=pltpu.VMEM)
    copies = 3 * PAIRS + ITERS * (3 + 2 * PIECES + 2 * (GROUP - 1) + RING - 1)
    vmem = pltpu.VMEM
    free, log_weight = pl.pallas_call(
        kernel,
        out_shape=tuple(jax.ShapeDtypeStruct((B, n), F32) for n in (KS, NS)),
        in_specs=[outside] * 4,
        out_specs=(inside,) * 2,
        scratch_shapes=[
            vmem((PIECES, KS, W), F32),
            vmem((PIECES, KS, W), BF16),
            vmem((PIECES, KS, W), BF16),
            vmem((GROUP, 128), jnp.int32),
            vmem((B, NS), jnp.int32),
            vmem((B, KS), F32),
            vmem((2 * B, KS), BF16),
            vmem((2, 2 * B, W), BF16),
            vmem((B, 128), F32),
            vmem((GROUP, 128), F32),
            vmem((ITERS, PIECES, B, W), F32),
            vmem((ITERS, PIECES, B, W), F32),
            vmem((ITERS, PIECES, B, W), F32),
            vmem((ITERS, PIECES, B, W), F32),
            vmem((ITERS, 1, 128), F32),
            vmem((ITERS, 3, 1, 128), F32),
            vmem((PAIRS, 2, 2 * W), F32),
            vmem((3, PAIRS, 2, 2 * W), F32),
            vmem((ITERS, GROUP, B + 8, 128), F32),
            vmem((ITERS, GROUP, B + 8, 128), F32),
            vmem((ITERS, B + 8, 128), F32),
            vmem((ITERS, RING, B + 8, 128), F32),
            vmem((ITERS, B, 128), F32),
            vmem((ITERS, GROUP, B, 128), F32),
            pltpu.SemaphoreType.DMA((PIECES,)),
            pltpu.SemaphoreType.DMA((3,)),
            pltpu.SemaphoreType.DMA((copies,)),
            pltpu.SemaphoreType.DMA((copies,)),
        ],
        compiler_params=pltpu.CompilerParams(
            collective_id=0, has_side_effects=True, vmem_limit_bytes=56 * 2**20
        ),
    )(energies, samples.reshape(GROUP, 128), counts, initial)
    return pl.pallas_call(
        finish,
        out_shape=(jax.ShapeDtypeStruct((B, KS), F32), jax.ShapeDtypeStruct((B, NS), F32)),
        in_specs=[outside] * 2,
        out_specs=(outside,) * 2,
        scratch_shapes=[vmem((B, KS), F32), vmem((B, NS), F32), pltpu.SemaphoreType.DMA((4,))],
    )(free, log_weight)


def solution(mesh):
    in_specs = (P("state", "conf"), P("state"), P(None, "conf"), P(None, "state"))
    out_specs = (P(None, "state"), P(None, "conf"))
    return jax.shard_map(
        per_device, mesh=mesh, in_specs=in_specs, out_specs=out_specs, check_vma=False
    )
```
